256 devices in a mesh: rows: 16 (over z, y_lo), cols: 16 (over y_hi, x, core).
Axes of the slice: x: 4, y: 4 (y_hi: 2, y_lo: 2; y = y_hi * 2 + y_lo), z: 8, core: 2. Of those that a mesh axis runs over, the one named last changes fastest.
Arguments:
- signal: float32 [32, 32, 64, 256], P(None, 'cols', 'rows'), may hold values from -6 to 6
- kernel: float32 [32, 32, 64, 256], P(None, 'cols', 'rows'), may hold values from -6 to 6
- gate_values: float32 [32, 32, 64, 256], P(None, 'cols', 'rows'), may hold values from -6 to 6
- grad_out: float32 [32, 32, 64, 256], P(None, 'cols', 'rows'), may hold values from -6 to 6
Outputs:
- gated: float32 [32, 32, 64, 256], P(None, 'cols', 'rows')
- signal_grad: float32 [32, 32, 64, 256], P(None, 'cols', 'rows')
- kernel_grad: float32 [32, 32, 64, 256], P(None, 'cols', 'rows')
- gate_grad: float32 [32, 32, 64, 256], P(None, 'cols', 'rows')
The draws below stay inside these ranges and needn't reach their ends.
All inputs are finite; a program needn't handle non-finite values.
Results may differ from the reference program's by a relative error of at most 0.000098.
Values sent between devices are 32-bit elements; how exact they have to be, the bound alone decides.
No kernel may reach another device: no remote copies, remote signals or barrier semaphores. Data moves between devices by JAX's collectives and lax.ppermute only.
A program may use at most 64 MiB of HBM per device.

```python
import math
import jax
import jax.numpy as jnp
from jax import lax

N1 = 32
N2 = 32
N3 = 64
CH = 256


def level_of(own_key, extent, split, low, top_value):
    gain, own = 1.0, jax.random.fold_in(own_key, 6)
    for dim, shards_of in split:
        draws = jnp.exp(jax.random.uniform(jax.random.fold_in(own, dim), (shards_of,), jnp.float32, low / len(split), top_value / len(split)))
        gain = gain * jnp.repeat(draws, extent[dim] // shards_of).reshape([-1 if axis == dim else 1 for axis in range(len(extent))])
    return gain


def noise(key, shape, spread, bound, split=(), dtype=jnp.bfloat16):
    values = jax.random.normal(key, shape, jnp.float32) * spread
    if len(split) > 0:
        values = level_of(key, shape, split, -0.22, 0.18) * values
    return jnp.clip(values, min=-bound, max=bound).astype(dtype)


def setup_inputs(seed: int = 0) -> dict:
    keys = jax.random.split(jax.random.key(seed), 5)
    signal = noise(keys[0], (N1, N2, N3, CH), 1.0, 6.0, ((1, 16), (2, 16)), jnp.float32)
    kernel = noise(keys[1], (N1, N2, N3, CH), 1.0, 6.0, ((1, 16), (2, 16)), jnp.float32)
    gate_values = noise(keys[2], (N1, N2, N3, CH), 1.0, 6.0, ((1, 16), (2, 16)), jnp.float32)
    grad_out = noise(keys[3], (N1, N2, N3, CH), 1.0, 6.0, ((1, 16), (2, 16)), jnp.float32)
    return {"signal": signal, "kernel": kernel, "gate_values": gate_values, "grad_out": grad_out}


def channel_block(pieces):
    signal, kernel, gate_values, grad_out = pieces
    positions = signal.shape[0]
    norm_scale = 1.0 / math.sqrt(positions)
    sig_spec = jnp.fft.rfft(signal, axis=0)
    ker_spec = jnp.fft.rfft(kernel, axis=0)
    convolved = jnp.fft.irfft(sig_spec * ker_spec, n=positions, axis=0) * norm_scale
    conv_grad = grad_out * gate_values
    grad_spec = jnp.fft.rfft(conv_grad, axis=0)
    signal_grad = jnp.fft.irfft(grad_spec * jnp.conj(ker_spec), n=positions, axis=0) * norm_scale
    kernel_grad = jnp.fft.irfft(grad_spec * jnp.conj(sig_spec), n=positions, axis=0) * norm_scale
    return (gate_values * convolved, signal_grad, kernel_grad, grad_out * convolved)

def reference(signal, kernel, gate_values, grad_out):
    positions = N1 * N2 * N3
    groups = CH // 32

    def to_blocks(array):
        return array.reshape(positions, groups, 32).transpose(1, 0, 2)

    def from_blocks(array):
        return array.transpose(1, 0, 2).reshape(N1, N2, N3, CH)
    results = lax.map(channel_block, (to_blocks(signal), to_blocks(kernel), to_blocks(gate_values), to_blocks(grad_out)))
    return (from_blocks(results[0]), from_blocks(results[1]), from_blocks(results[2]), from_blocks(results[3]))
```

```python
import functools

import jax
import jax.numpy as jnp
import ml_dtypes
import numpy as np
from jax import lax
from jax.experimental import pallas as pl
from jax.experimental.pallas import tpu as pltpu
from jax.sharding import PartitionSpec as P

LENGTH = 65536
LANES = 128
FIELDS = 3
ROWS = 56
SCALE = 1.0 / (65536.0 * 256.0)
HALF = jnp.bfloat16


def halves(table):
    high = table.astype(np.float32).astype(ml_dtypes.bfloat16)
    low = (table - high.astype(np.float64)).astype(np.float32).astype(ml_dtypes.bfloat16)
    return high, low


@functools.lru_cache(maxsize=None)
def tables():
    a = np.arange(32)
    fa = np.arange(16)
    angle = 2.0 * np.pi * (fa[:, None] * a[None, :] % 32) / 32.0
    first = np.zeros((144, 128))
    last = np.zeros((144, 128))
    weight = np.where(fa == 0, 1.0, 2.0)[:, None] * SCALE
    for cl in range(4):
        columns = slice(32 * cl, 32 * cl + 32)
        first[16 * cl : 16 * cl + 16, columns] = np.cos(angle)
        first[64 + 16 * cl : 64 + 16 * cl + 16, columns] = -np.sin(angle)
        first[128 + cl, columns] = np.where(a % 2 == 0, 1.0, -1.0)
        last[16 * cl : 16 * cl + 16, columns] = weight * np.cos(angle)
        last[64 + 16 * cl : 64 + 16 * cl + 16, columns] = -weight * np.sin(angle)
        last[128 + cl, columns] = np.where(a % 2 == 0, SCALE, -SCALE)
    lane = np.arange(256)
    m = 16 * (lane % 16) + 8 * (lane // 128) + (lane // 16) % 8
    g0 = np.arange(256)
    middle = 2.0 * np.pi * (m[:, None] * g0[None, :] % 256) / 256.0
    forward = np.concatenate([np.cos(middle), np.sin(middle)], axis=1)
    backward = np.concatenate([np.cos(middle).T, np.sin(middle).T], axis=1)
    fa = np.arange(17)
    phase = 2.0 * np.pi * (8 * fa[:, None] * m[None, :] % LENGTH) / LENGTH
    turn_m = np.zeros((2, 24, 256), np.float32)
    turn_m[0, :17] = np.cos(phase)
    turn_m[1, :17] = np.sin(phase)
    c8 = np.arange(8)
    phase = c8[:, None, None] * (fa[None, :, None] + 32 * g0[None, None, :]) % LENGTH
    phase = 2.0 * np.pi * phase / LENGTH
    turn_c = np.zeros((2, 8, 24, 256), np.float32)
    turn_c[0, :, :17] = np.cos(phase)
    turn_c[1, :, :17] = np.sin(phase)
    return (*halves(first), *halves(forward), *halves(backward), *halves(last), turn_m, turn_c)


def split(values):
    high = values.astype(HALF)
    return high, (values - high.astype(jnp.float32)).astype(HALF)


def product(left, right, dims):
    def one(x, y):
        return lax.dot_general(x, y, (dims, ((), ())), preferred_element_type=jnp.float32)

    return one(left[0], right[0]) + (one(left[0], right[1]) + one(left[1], right[0]))


def eight(values, sign):
    def add(x, y):
        return (x[0] + y[0], x[1] + y[1])

    def sub(x, y):
        return (x[0] - y[0], x[1] - y[1])

    def quarter(x):
        return (-sign * x[1], sign * x[0])

    def four(v):
        s, d = add(v[0], v[2]), sub(v[0], v[2])
        t, u = add(v[1], v[3]), quarter(sub(v[1], v[3]))
        return [add(s, t), add(d, u), sub(s, t), sub(d, u)]

    root = float(np.sqrt(0.5))
    even, odd = four(values[0::2]), four(values[1::2])
    x = odd[1]
    odd[1] = (root * (x[0] - sign * x[1]), root * (x[1] + sign * x[0]))
    odd[2] = quarter(odd[2])
    x = odd[3]
    odd[3] = (root * (-x[0] - sign * x[1]), root * (-x[1] + sign * x[0]))
    return [add(x, y) for x, y in zip(even, odd)] + [sub(x, y) for x, y in zip(even, odd)]


def times(x, y):
    return (x[0] * y[0] - x[1] * y[1], x[0] * y[1] + x[1] * y[0])


def times_conj(x, y):
    return (x[0] * y[0] + x[1] * y[1], x[1] * y[0] - x[0] * y[1])


def pack_kernel(signal, kernel, gate, grad, out):
    for field in range(FIELDS):
        for half in range(2):
            for bl in range(2):
                parts = []
                for cl in range(4):
                    rows = pl.ds(bl * 8 + half * 4 + cl, 32, stride=16)
                    if field == 0:
                        parts.append(signal[rows, :])
                    elif field == 1:
                        parts.append(kernel[rows, :])
                    else:
                        parts.append(gate[rows, :] * grad[rows, :])
                block = jnp.concatenate(parts, axis=0).T
                out[pl.ds(half * 768 + field * 2 + bl, 128, stride=6), :] = block


def unpack_kernel(arrived, gate, grad, gated, signal_grad, kernel_grad, gate_grad):
    for field in range(FIELDS):
        for half in range(2):
            for bl in range(2):
                block = arrived[pl.ds(half * 768 + field * 2 + bl, 128, stride=6), :].T
                for cl in range(4):
                    rows = pl.ds(bl * 8 + half * 4 + cl, 32, stride=16)
                    part = block[32 * cl : 32 * cl + 32]
                    if field == 0:
                        gated[rows, :] = gate[rows, :] * part
                        gate_grad[rows, :] = grad[rows, :] * part
                    elif field == 1:
                        signal_grad[rows, :] = part
                    else:
                        kernel_grad[rows, :] = part


def channel_kernel(
    arrived, first_hi, first_lo, forward_hi, forward_lo, backward_hi, backward_lo,
    last_hi, last_lo, turn_m, turn_c, out, real, imag,
):
    pad = jnp.zeros((8, ROWS - 48, 256), jnp.float32)
    real[:, 48:ROWS, :] = pad
    imag[:, 48:ROWS, :] = pad
    cos_m, sin_m = turn_m[0, 0:16], turn_m[1, 0:16]
    cos_x, sin_x = turn_m[0, 16:17], turn_m[1, 16:17]
    first = (first_hi[...], first_lo[...])
    for field in range(FIELDS):
        blocks = [
            arrived[pl.ds(field * 2 + bl, 256, stride=6), :].reshape(8, 2, 16, 128) for bl in range(2)
        ]
        for e in range(2):
            block = jnp.concatenate([b[:, e].reshape(128, 128) for b in blocks], axis=0)
            mixed = product(first, split(block), ((1,), (1,)))
            for cl in range(4):
                c8 = 4 * e + cl
                x, y = mixed[16 * cl : 16 * cl + 16], mixed[64 + 16 * cl : 80 + 16 * cl]
                real[c8, 16 * field : 16 * field + 16, :] = x * cos_m + y * sin_m
                imag[c8, 16 * field : 16 * field + 16, :] = y * cos_m - x * sin_m
                x = mixed[128 + cl : 129 + cl]
                real[c8, 48 + field : 49 + field, :] = x * cos_x
                imag[c8, 48 + field : 49 + field, :] = -(x * sin_x)

    def along_lanes(table, sign):
        x = split(real[...].reshape(8 * ROWS, 256))
        y = split(imag[...].reshape(8 * ROWS, 256))
        x = product(x, table, ((1,), (0,)))
        y = product(y, table, ((1,), (0,)))
        real[...] = (x[:, :256] - sign * y[:, 256:]).reshape(8, ROWS, 256)
        imag[...] = (y[:, :256] + sign * x[:, 256:]).reshape(8, ROWS, 256)

    along_lanes((forward_hi[...], forward_lo[...]), -1.0)
    for rows_of, turns in (
        ([slice(16 * f, 16 * f + 8) for f in range(3)], slice(0, 8)),
        ([slice(16 * f + 8, 16 * f + 16) for f in range(3)], slice(8, 16)),
        ([slice(48 + f, 49 + f) for f in range(3)], slice(16, 17)),
    ):
        for lanes in (slice(0, 128), slice(128, 256)):
            turn = [(turn_c[0, c8, turns, lanes], turn_c[1, c8, turns, lanes]) for c8 in range(8)]
            spectra = []
            for rows in rows_of:
                values = [(real[c8, rows, lanes], imag[c8, rows, lanes]) for c8 in range(8)]
                spectra.append(eight([times_conj(v, t) for v, t in zip(values, turn)], -1.0))
            results = (
                [times(s, k) for s, k in zip(spectra[0], spectra[1])],
                [times_conj(g, k) for g, k in zip(spectra[2], spectra[1])],
                [times_conj(g, s) for g, s in zip(spectra[2], spectra[0])],
            )
            for rows, result in zip(rows_of, results):
                for c8, (v, t) in enumerate(zip(eight(result, 1.0), turn)):
                    v = times(v, t)
                    real[c8, rows, lanes] = v[0]
                    imag[c8, rows, lanes] = v[1]
    along_lanes((backward_hi[...], backward_lo[...]), 1.0)

    last = (last_hi[...], last_lo[...])
    fill = jnp.zeros((12, 256), jnp.float32)
    for field in range(FIELDS):
        done = []
        for e in range(2):
            reals, imags, extra = [], [], []
            for cl in range(4):
                c8 = 4 * e + cl
                x = real[c8, 16 * field : 16 * field + 16, :]
                y = imag[c8, 16 * field : 16 * field + 16, :]
                reals.append(x * cos_m - y * sin_m)
                imags.append(y * cos_m + x * sin_m)
                x, y = real[c8, 48 + field : 49 + field, :], imag[c8, 48 + field : 49 + field, :]
                extra.append(x * cos_x - y * sin_x)
            mixed = jnp.concatenate(reals + imags + extra + [fill], axis=0)
            done.append(product(split(mixed), last, ((0,), (0,))))
        for bl in range(2):
            pair = [d[128 * bl : 128 * bl + 128].reshape(8, 1, 16, 128) for d in done]
            block = jnp.concatenate(pair, axis=1).reshape(256, 128)
            out[pl.ds(field * 2 + bl, 256, stride=6), :] = block


VMEM = pl.BlockSpec(memory_space=pltpu.VMEM)


def call(body, operands, shapes, scratch=(), limit=32 << 20, flops=10**6):
    return pl.pallas_call(
        body,
        out_shape=shapes,
        in_specs=[VMEM] * len(operands),
        out_specs=jax.tree.map(lambda _: VMEM, shapes),
        scratch_shapes=scratch,
        compiler_params=pltpu.CompilerParams(vmem_limit_bytes=limit),
    )(*operands)


def flat(x):
    return x.reshape(32, 2, 4, 2, LANES).transpose(0, 1, 3, 2, 4).reshape(512, LANES)


def unflat(x):
    return x.reshape(32, 2, 2, 4, LANES).transpose(0, 1, 3, 2, 4).reshape(32, 2, 4, 256)


def exchange(x):
    x = x.reshape(256, FIELDS, 2, LANES)
    x = lax.all_to_all(x, ("rows", "cols"), split_axis=0, concat_axis=0, tiled=True)
    return x.reshape(256 * FIELDS * 2, LANES)


def shards(signal, kernel, gate_values, grad_out):
    signal, kernel, gate, grad = (flat(x) for x in (signal, kernel, gate_values, grad_out))
    wide = jax.ShapeDtypeStruct((1536, LANES), jnp.float32)
    own = jax.ShapeDtypeStruct((512, LANES), jnp.float32)
    packed = call(pack_kernel, (signal, kernel, gate, grad), wide)
    arrived = exchange(packed)
    scratch = [pltpu.VMEM((8, ROWS, 256), jnp.float32)] * 2
    done = call(channel_kernel, (arrived, *tables()), wide, scratch)
    results = call(unpack_kernel, (exchange(done), gate, grad), (own,) * 4)
    return tuple(unflat(x) for x in results)


def solution(mesh):
    place = P(None, "cols", "rows", None)
    return jax.shard_map(
        shards, mesh=mesh, in_specs=(place,) * 4, out_specs=(place,) * 4, check_vma=False
    )
```

```python
import functools

import jax
import jax.numpy as jnp
import ml_dtypes
import numpy as np
from jax import lax
from jax.experimental import pallas as pl
from jax.experimental.pallas import tpu as pltpu
from jax.sharding import PartitionSpec as P

LENGTH = 65536
LANES = 128
FIELDS = 3
ROWS = 56
SCALE = 1.0 / (65536.0 * 256.0)
HALF = jnp.bfloat16


def halves(table):
    high = table.astype(np.float32).astype(ml_dtypes.bfloat16)
    low = (table - high.astype(np.float64)).astype(np.float32).astype(ml_dtypes.bfloat16)
    return high, low


def tall(table):
    return np.concatenate(np.split(table, 4, axis=1))


@functools.lru_cache(maxsize=None)
def tables():
    a = np.arange(32)
    fa = np.arange(16)
    angle = 2.0 * np.pi * (fa[:, None] * a[None, :] % 32) / 32.0
    first = np.zeros((144, 128))
    last = np.zeros((144, 128))
    weight = np.where(fa == 0, 1.0, 2.0)[:, None] * SCALE
    for cl in range(4):
        columns = slice(32 * cl, 32 * cl + 32)
        first[16 * cl : 16 * cl + 16, columns] = np.cos(angle)
        first[64 + 16 * cl : 64 + 16 * cl + 16, columns] = -np.sin(angle)
        first[128 + cl, columns] = np.where(a % 2 == 0, 1.0, -1.0)
        last[16 * cl : 16 * cl + 16, columns] = weight * np.cos(angle)
        last[64 + 16 * cl : 64 + 16 * cl + 16, columns] = -weight * np.sin(angle)
        last[128 + cl, columns] = np.where(a % 2 == 0, SCALE, -SCALE)
    lane = np.arange(256)
    m = 16 * (lane % 16) + 8 * (lane // 128) + (lane // 16) % 8
    g0 = np.arange(256)
    middle = 2.0 * np.pi * (m[:, None] * g0[None, :] % 256) / 256.0
    forward = np.concatenate([np.cos(middle), np.sin(middle)], axis=1)
    backward = np.concatenate([np.cos(middle).T, np.sin(middle).T], axis=1)
    fa = np.arange(17)
    phase = 2.0 * np.pi * (8 * fa[:, None] * m[None, :] % LENGTH) / LENGTH
    turn_m = np.zeros((2, 24, 256), np.float32)
    turn_m[0, :17] = np.cos(phase)
    turn_m[1, :17] = np.sin(phase)
    c8 = np.arange(8)
    phase = c8[:, None, None] * (fa[None, :, None] + 32 * g0[None, None, :]) % LENGTH
    phase = 2.0 * np.pi * phase / LENGTH
    turn_c = np.zeros((2, 8, 24, 256), np.float32)
    turn_c[0, :, :17] = np.cos(phase)
    turn_c[1, :, :17] = np.sin(phase)
    return (*halves(first), *halves(tall(forward)), *halves(tall(backward)), *halves(last), turn_m, turn_c)


def split(values):
    high = values.astype(HALF)
    return high, (values - high.astype(jnp.float32)).astype(HALF)


def product(left, right, dims):
    def one(x, y):
        return lax.dot_general(x, y, (dims, ((), ())), preferred_element_type=jnp.float32)

    return one(left[0], right[0]) + (one(left[0], right[1]) + one(left[1], right[0]))


def eight(values, sign):
    def add(x, y):
        return (x[0] + y[0], x[1] + y[1])

    def sub(x, y):
        return (x[0] - y[0], x[1] - y[1])

    def quarter(x):
        return (-sign * x[1], sign * x[0])

    def four(v):
        s, d = add(v[0], v[2]), sub(v[0], v[2])
        t, u = add(v[1], v[3]), quarter(sub(v[1], v[3]))
        return [add(s, t), add(d, u), sub(s, t), sub(d, u)]

    root = float(np.sqrt(0.5))
    even, odd = four(values[0::2]), four(values[1::2])
    x = odd[1]
    odd[1] = (root * (x[0] - sign * x[1]), root * (x[1] + sign * x[0]))
    odd[2] = quarter(odd[2])
    x = odd[3]
    odd[3] = (root * (-x[0] - sign * x[1]), root * (-x[1] + sign * x[0]))
    return [add(x, y) for x, y in zip(even, odd)] + [sub(x, y) for x, y in zip(even, odd)]


def times(x, y):
    return (x[0] * y[0] - x[1] * y[1], x[0] * y[1] + x[1] * y[0])


def times_conj(x, y):
    return (x[0] * y[0] + x[1] * y[1], x[1] * y[0] - x[0] * y[1])


def pack_kernel(signal, kernel, gate, grad, out, signal_v, kernel_v, gate_v, grad_v, done):
    copies = []
    for k, (source, target) in enumerate(
        ((signal, signal_v), (kernel, kernel_v), (gate, gate_v), (grad, grad_v))
    ):
        for part in range(4):
            rows = pl.ds(128 * part, 128)
            copies.append(pltpu.make_async_copy(source.at[rows], target.at[rows], done.at[4 * k + part]))
    for copy in copies:
        copy.start()
    for field in range(FIELDS):
        for copy in copies[4 * field : 4 * field + 4] if field < 2 else copies[8:]:
            copy.wait()
        for half in range(2):
            for bl in range(2):
                parts = []
                for cl in range(4):
                    rows = pl.ds(bl * 8 + half * 4 + cl, 32, stride=16)
                    if field == 0:
                        parts.append(signal_v[rows, :])
                    elif field == 1:
                        parts.append(kernel_v[rows, :])
                    else:
                        parts.append(gate_v[rows, :] * grad_v[rows, :])
                block = jnp.concatenate(parts, axis=0).T
                out[pl.ds(768 * half + field * 2 + bl, 128, stride=6), :] = block


def unpack_kernel(arrived, gate, grad, gated, signal_grad, kernel_grad, gate_grad):
    for field in range(FIELDS):
        for bl in range(2):
            for half in range(2):
                block = arrived[pl.ds(768 * half + field * 2 + bl, 128, stride=6), :].T
                for cl in range(4):
                    rows = pl.ds(bl * 8 + half * 4 + cl, 32, stride=16)
                    part = block[32 * cl : 32 * cl + 32]
                    if field == 0:
                        gated[rows, :] = gate[rows, :] * part
                        gate_grad[rows, :] = grad[rows, :] * part
                    elif field == 1:
                        signal_grad[rows, :] = part
                    else:
                        kernel_grad[rows, :] = part


def channel_kernel(
    arrived, first_hi, first_lo, forward_hi, forward_lo, backward_hi, backward_lo,
    last_hi, last_lo, turn_m, turn_c, out, real, imag,
):
    pad = jnp.zeros((8, ROWS - 48, 256), jnp.float32)
    real[:, 48:ROWS, :] = pad
    imag[:, 48:ROWS, :] = pad
    cos_m, sin_m = turn_m[0, 0:16], turn_m[1, 0:16]
    cos_x, sin_x = turn_m[0, 16:17], turn_m[1, 16:17]
    first = (first_hi[...], first_lo[...])
    for field in range(FIELDS):
        blocks = [
            arrived[pl.ds(field * 2 + bl, 256, stride=6), :].reshape(8, 2, 16, 128) for bl in range(2)
        ]
        for e in range(2):
            block = jnp.concatenate([b[:, e].reshape(128, 128) for b in blocks], axis=0)
            mixed = product(first, split(block), ((1,), (1,)))
            for cl in range(4):
                c8 = 4 * e + cl
                x, y = mixed[16 * cl : 16 * cl + 16], mixed[64 + 16 * cl : 80 + 16 * cl]
                real[c8, 16 * field : 16 * field + 16, :] = x * cos_m + y * sin_m
                imag[c8, 16 * field : 16 * field + 16, :] = y * cos_m - x * sin_m
                x = mixed[128 + cl : 129 + cl]
                real[c8, 48 + field : 49 + field, :] = x * cos_x
                imag[c8, 48 + field : 49 + field, :] = -(x * sin_x)

    def along_lanes(table, sign):
        x = split(real[...].reshape(8 * ROWS, 256))
        y = split(imag[...].reshape(8 * ROWS, 256))
        table = [jnp.concatenate([t[256 * k : 256 * k + 256, :] for k in range(4)], axis=1) for t in table]
        x = product(x, table, ((1,), (0,)))
        y = product(y, table, ((1,), (0,)))
        real[...] = (x[:, :256] - sign * y[:, 256:]).reshape(8, ROWS, 256)
        imag[...] = (y[:, :256] + sign * x[:, 256:]).reshape(8, ROWS, 256)

    along_lanes((forward_hi, forward_lo), -1.0)
    for rows_of, turns in (
        ([slice(16 * f, 16 * f + 8) for f in range(3)], slice(0, 8)),
        ([slice(16 * f + 8, 16 * f + 16) for f in range(3)], slice(8, 16)),
        ([slice(48 + f, 49 + f) for f in range(3)], slice(16, 17)),
    ):
        for lanes in (slice(0, 128), slice(128, 256)):
            turn = [(turn_c[0, c8, turns, lanes], turn_c[1, c8, turns, lanes]) for c8 in range(8)]
            spectra = []
            for rows in rows_of:
                values = [(real[c8, rows, lanes], imag[c8, rows, lanes]) for c8 in range(8)]
                spectra.append(eight([times_conj(v, t) for v, t in zip(values, turn)], -1.0))
            results = (
                [times(s, k) for s, k in zip(spectra[0], spectra[1])],
                [times_conj(g, k) for g, k in zip(spectra[2], spectra[1])],
                [times_conj(g, s) for g, s in zip(spectra[2], spectra[0])],
            )
            for rows, result in zip(rows_of, results):
                for c8, (v, t) in enumerate(zip(eight(result, 1.0), turn)):
                    v = times(v, t)
                    real[c8, rows, lanes] = v[0]
                    imag[c8, rows, lanes] = v[1]
    along_lanes((backward_hi, backward_lo), 1.0)

    last = (last_hi[...], last_lo[...])
    fill = jnp.zeros((12, 256), jnp.float32)
    for field in range(FIELDS):
        done = []
        for e in range(2):
            reals, imags, extra = [], [], []
            for cl in range(4):
                c8 = 4 * e + cl
                x = real[c8, 16 * field : 16 * field + 16, :]
                y = imag[c8, 16 * field : 16 * field + 16, :]
                reals.append(x * cos_m - y * sin_m)
                imags.append(y * cos_m + x * sin_m)
                x, y = real[c8, 48 + field : 49 + field, :], imag[c8, 48 + field : 49 + field, :]
                extra.append(x * cos_x - y * sin_x)
            mixed = jnp.concatenate(reals + imags + extra + [fill], axis=0)
            done.append(product(split(mixed), last, ((0,), (0,))))
        for bl in range(2):
            pair = [d[128 * bl : 128 * bl + 128].reshape(8, 1, 16, 128) for d in done]
            block = jnp.concatenate(pair, axis=1).reshape(256, 128)
            out[pl.ds(field * 2 + bl, 256, stride=6), :] = block


VMEM = pl.BlockSpec(memory_space=pltpu.VMEM)
HBM = pl.BlockSpec(memory_space=pltpu.HBM)


def call(body, operands, in_specs, shapes, out_specs, scratch=(), limit=24 << 20):
    return pl.pallas_call(
        body,
        out_shape=shapes,
        in_specs=in_specs,
        out_specs=out_specs,
        scratch_shapes=scratch,
        compiler_params=pltpu.CompilerParams(vmem_limit_bytes=limit),
    )(*operands)


WIDE = jax.ShapeDtypeStruct((1536, LANES), jnp.float32)
OWN = jax.ShapeDtypeStruct((512, LANES), jnp.float32)
WHOLE = [pltpu.VMEM((512, LANES), jnp.float32)] * 4 + [pltpu.SemaphoreType.DMA((16,))]


def run_pack(signal, kernel, gate, grad):
    return call(pack_kernel, (signal, kernel, gate, grad), [HBM] * 4, WIDE, VMEM, WHOLE)


def run_channel(arrived):
    constants = tables()
    scratch = [pltpu.VMEM((8, ROWS, 256), jnp.float32)] * 2
    specs = [VMEM] * (1 + len(constants))
    return call(channel_kernel, (arrived, *constants), specs, WIDE, VMEM, scratch)


def run_unpack(arrived, gate, grad):
    return call(unpack_kernel, (arrived, gate, grad), [VMEM] * 3, (OWN,) * 4, (VMEM,) * 4)


def flat(x):
    return x.reshape(32, 2, 4, 2, LANES).transpose(0, 1, 3, 2, 4).reshape(512, LANES)


def unflat(x):
    return x.reshape(32, 2, 2, 4, LANES).transpose(0, 1, 3, 2, 4).reshape(32, 2, 4, 256)


def exchange(x):
    x = x.reshape(256, FIELDS, 2, LANES)
    x = lax.all_to_all(x, ("rows", "cols"), split_axis=0, concat_axis=0, tiled=True)
    return x.reshape(1536, LANES)


def shards(signal, kernel, gate_values, grad_out):
    inputs = [flat(x) for x in (signal, kernel, gate_values, grad_out)]
    stored = [pltpu.with_memory_space_constraint(x, pltpu.HBM) for x in inputs]
    done = exchange(run_channel(exchange(run_pack(*stored))))
    return tuple(unflat(x) for x in run_unpack(done, *inputs[2:]))


def solution(mesh):
    place = P(None, "cols", "rows", None)
    return jax.shard_map(
        shards, mesh=mesh, in_specs=(place,) * 4, out_specs=(place,) * 4, check_vma=False
    )
```

```python
import functools

import jax
import jax.numpy as jnp
import ml_dtypes
import numpy as np
from jax import lax
from jax.experimental import pallas as pl
from jax.experimental.pallas import tpu as pltpu
from jax.sharding import PartitionSpec as P

LENGTH = 65536
LANES = 128
FIELDS = 3
EXTRA = 384
ROWS = EXTRA + 32
SCALE = 1.0 / (65536.0 * 256.0)
HALF = jnp.bfloat16


def halves(table):
    high = table.astype(np.float32).astype(ml_dtypes.bfloat16)
    low = (table - high.astype(np.float64)).astype(np.float32).astype(ml_dtypes.bfloat16)
    return high, low


def tall(table):
    return np.concatenate(np.split(table, 4, axis=1))


@functools.lru_cache(maxsize=None)
def tables():
    a = np.arange(32)
    fa = np.arange(16)
    angle = 2.0 * np.pi * (fa[:, None] * a[None, :] % 32) / 32.0
    first = np.zeros((144, 128))
    last = np.zeros((128, 128))
    weight = np.where(fa == 0, 1.0, 2.0)[:, None] * SCALE
    for cl in range(4):
        columns = slice(32 * cl, 32 * cl + 32)
        first[16 * cl : 16 * cl + 16, columns] = np.cos(angle)
        first[64 + 16 * cl : 64 + 16 * cl + 16, columns] = -np.sin(angle)
        first[128 + cl, columns] = np.where(a % 2 == 0, 1.0, -1.0)
        last[16 * cl : 16 * cl + 16, columns] = weight * np.cos(angle)
        last[64 + 16 * cl : 64 + 16 * cl + 16, columns] = -weight * np.sin(angle)
        last[64 + 16 * cl, columns] = np.where(a % 2 == 0, SCALE, -SCALE)
    lane = np.arange(256)
    m = 16 * (lane % 16) + 8 * (lane // 128) + (lane // 16) % 8
    g0 = np.arange(256)
    middle = 2.0 * np.pi * (m[:, None] * g0[None, :] % 256) / 256.0
    forward = np.concatenate([np.cos(middle), np.sin(middle)], axis=1)
    backward = np.concatenate([np.cos(middle).T, np.sin(middle).T], axis=1)
    fa = np.arange(17)
    phase = 2.0 * np.pi * (8 * fa[:, None] * m[None, :] % LENGTH) / LENGTH
    turn_m = np.zeros((2, 24, 256), np.float32)
    turn_m[0, :17] = np.cos(phase)
    turn_m[1, :17] = np.sin(phase)
    c8 = np.arange(8)
    phase = c8[:, None, None] * (fa[None, :, None] + 32 * g0[None, None, :]) % LENGTH
    phase = 2.0 * np.pi * phase / LENGTH
    turn_c = np.zeros((2, 8, 24, 256), np.float32)
    turn_c[0, :, :17] = np.cos(phase)
    turn_c[1, :, :17] = np.sin(phase)
    return (*halves(first), *halves(tall(forward)), *halves(tall(backward)), turn_m, turn_c, *halves(last.T))


def split(values):
    high = values.astype(HALF)
    return high, (values - high.astype(jnp.float32)).astype(HALF)


def product(left, right, dims):
    def one(x, y):
        return lax.dot_general(x, y, (dims, ((), ())), preferred_element_type=jnp.float32)

    return one(left[0], right[0]) + (one(left[0], right[1]) + one(left[1], right[0]))


def eight(values, sign):
    def add(x, y):
        return (x[0] + y[0], x[1] + y[1])

    def sub(x, y):
        return (x[0] - y[0], x[1] - y[1])

    def quarter(x):
        return (-sign * x[1], sign * x[0])

    def four(v):
        s, d = add(v[0], v[2]), sub(v[0], v[2])
        t, u = add(v[1], v[3]), quarter(sub(v[1], v[3]))
        return [add(s, t), add(d, u), sub(s, t), sub(d, u)]

    root = float(np.sqrt(0.5))
    even, odd = four(values[0::2]), four(values[1::2])
    x = odd[1]
    odd[1] = (root * (x[0] - sign * x[1]), root * (x[1] + sign * x[0]))
    odd[2] = quarter(odd[2])
    x = odd[3]
    odd[3] = (root * (-x[0] - sign * x[1]), root * (-x[1] + sign * x[0]))
    return [add(x, y) for x, y in zip(even, odd)] + [sub(x, y) for x, y in zip(even, odd)]


def times(x, y):
    return (x[0] * y[0] - x[1] * y[1], x[0] * y[1] + x[1] * y[0])


def times_conj(x, y):
    return (x[0] * y[0] + x[1] * y[1], x[1] * y[0] - x[0] * y[1])


def pack_kernel(signal, kernel, gate, grad, out):
    for field in range(FIELDS):
        for half in range(2):
            for bl in range(2):
                parts = []
                for cl in range(4):
                    rows = pl.ds(bl * 8 + half * 4 + cl, 32, stride=16)
                    if field == 0:
                        parts.append(signal[rows, :])
                    elif field == 1:
                        parts.append(kernel[rows, :])
                    else:
                        parts.append(gate[rows, :] * grad[rows, :])
                block = jnp.concatenate(parts, axis=0).T
                out[pl.ds(768 * half + field * 2 + bl, 128, stride=6), :] = block


def unpack_kernel(arrived, last_hi, last_lo, gate, grad, gated, signal_grad, kernel_grad, gate_grad):
    last = (last_hi[...], last_lo[...])
    for field in range(FIELDS):
        for bl in range(2):
            block = arrived[pl.ds(field * 2 + bl, 256, stride=6), :]
            block = product(last, split(block), ((1,), (1,)))
            for half in range(2):
                for cl in range(4):
                    rows = pl.ds(bl * 8 + half * 4 + cl, 32, stride=16)
                    part = block[32 * cl : 32 * cl + 32, 128 * half : 128 * half + 128]
                    if field == 0:
                        gated[rows, :] = gate[rows, :] * part
                        gate_grad[rows, :] = grad[rows, :] * part
                    elif field == 1:
                        signal_grad[rows, :] = part
                    else:
                        kernel_grad[rows, :] = part


def channel_kernel(
    arrived, first_hi, first_lo, forward_hi, forward_lo, backward_hi, backward_lo, turn_m, turn_c,
    out, real, imag,
):
    cos_m, sin_m = turn_m[0, 0:16], turn_m[1, 0:16]
    cos_x, sin_x = turn_m[0, 16:17], turn_m[1, 16:17]
    first = (first_hi[...], first_lo[...])
    pad = jnp.zeros((8, 256), jnp.float32)
    real[EXTRA + 24 :, :] = pad
    imag[EXTRA + 24 :, :] = pad
    for field in range(FIELDS):
        blocks = [
            arrived[pl.ds(field * 2 + bl, 256, stride=6), :].reshape(8, 2, 16, 128) for bl in range(2)
        ]
        for e in range(2):
            block = jnp.concatenate([b[:, e].reshape(128, 128) for b in blocks], axis=0)
            mixed = product(first, split(block), ((1,), (1,)))
            for cl in range(4):
                rows = pl.ds(48 * (4 * e + cl) + 16 * field, 16)
                x, y = mixed[16 * cl : 16 * cl + 16], mixed[64 + 16 * cl : 80 + 16 * cl]
                real[rows, :] = x * cos_m + y * sin_m
                imag[rows, :] = y * cos_m - x * sin_m
            rows = pl.ds(EXTRA + 8 * field + 4 * e, 4)
            x = mixed[128:132]
            real[rows, :] = x * cos_x
            imag[rows, :] = -(x * sin_x)

    def along_lanes(refs, sign, source, target):
        table = [jnp.concatenate([ref[256 * k : 256 * k + 256, :] for k in range(4)], axis=1) for ref in refs]
        start = 0
        for size in (208, 208):
            rows = pl.ds(start, size)
            start += size
            x = product(split(source[0][rows, :]), table, ((1,), (0,)))
            y = product(split(source[1][rows, :]), table, ((1,), (0,)))
            if sign < 0:
                target[0][rows, :] = x[:, :256] + y[:, 256:]
                target[1][rows, :] = y[:, :256] - x[:, 256:]
            else:
                target[0][rows, :] = x[:, :256] - y[:, 256:]
                target[1][rows, :] = y[:, :256] + x[:, 256:]

    along_lanes((forward_hi, forward_lo), -1, (real, imag), (real, imag))
    for start, pitch, count, step, turns in (
        (0, 48, 8, 16, slice(0, 8)),
        (8, 48, 8, 16, slice(8, 16)),
        (EXTRA, 1, 1, 8, slice(16, 17)),
    ):
        for lanes in (slice(0, 128), slice(128, 256)):
            turn = [(turn_c[0, c8, turns, lanes], turn_c[1, c8, turns, lanes]) for c8 in range(8)]
            spectra = []
            for field in range(FIELDS):
                rows = [pl.ds(start + step * field + pitch * c8, count) for c8 in range(8)]
                values = [(real[r, lanes], imag[r, lanes]) for r in rows]
                spectra.append(eight([times_conj(v, t) for v, t in zip(values, turn)], -1.0))
            results = (
                [times(s, k) for s, k in zip(spectra[0], spectra[1])],
                [times_conj(g, k) for g, k in zip(spectra[2], spectra[1])],
                [times_conj(g, s) for g, s in zip(spectra[2], spectra[0])],
            )
            for field, result in enumerate(results):
                for c8, (v, t) in enumerate(zip(eight(result, 1.0), turn)):
                    rows = pl.ds(start + step * field + pitch * c8, count)
                    real[rows, lanes], imag[rows, lanes] = times(v, t)
    along_lanes((backward_hi, backward_lo), 1, (real, imag), (real, imag))

    lead = lax.broadcasted_iota(jnp.int32, (16, 256), 0) == 0
    for field in range(FIELDS):
        done = []
        for e in range(2):
            rows = pl.ds(EXTRA + 8 * field + 4 * e, 4)
            extra = real[rows, :] * cos_x - imag[rows, :] * sin_x
            reals, imags = [], []
            for cl in range(4):
                rows = pl.ds(48 * (4 * e + cl) + 16 * field, 16)
                x, y = real[rows, :], imag[rows, :]
                reals.append(x * cos_m - y * sin_m)
                imags.append(jnp.where(lead, extra[cl : cl + 1], y * cos_m + x * sin_m))
            done.append(jnp.concatenate(reals + imags, axis=0).T)
        for bl in range(2):
            pair = [d[128 * bl : 128 * bl + 128].reshape(8, 1, 16, 128) for d in done]
            block = jnp.concatenate(pair, axis=1).reshape(256, 128)
            out[pl.ds(field * 2 + bl, 256, stride=6), :] = block


VMEM = pl.BlockSpec(memory_space=pltpu.VMEM)


def call(body, operands, in_specs, shapes, out_specs, scratch=(), limit=24 << 20):
    return pl.pallas_call(
        body,
        out_shape=shapes,
        in_specs=in_specs,
        out_specs=out_specs,
        scratch_shapes=scratch,
        compiler_params=pltpu.CompilerParams(vmem_limit_bytes=limit),
    )(*operands)


WIDE = jax.ShapeDtypeStruct((1536, LANES), jnp.float32)
OWN = jax.ShapeDtypeStruct((512, LANES), jnp.float32)


def run_pack(signal, kernel, gate, grad):
    return call(pack_kernel, (signal, kernel, gate, grad), [VMEM] * 4, WIDE, VMEM)


def run_channel(arrived):
    constants = tables()[:-2]
    scratch = [pltpu.VMEM((ROWS, 256), jnp.float32)] * 2
    specs = [VMEM] * (1 + len(constants))
    return call(channel_kernel, (arrived, *constants), specs, WIDE, VMEM, scratch)


def run_unpack(arrived, gate, grad):
    operands = (arrived, *tables()[-2:], gate, grad)
    return call(unpack_kernel, operands, [VMEM] * 5, (OWN,) * 4, (VMEM,) * 4)


def flat(x):
    return x.reshape(32, 2, 4, 2, LANES).transpose(0, 1, 3, 2, 4).reshape(512, LANES)


def unflat(x):
    return x.reshape(32, 2, 2, 4, LANES).transpose(0, 1, 3, 2, 4).reshape(32, 2, 4, 256)


def exchange(x):
    x = x.reshape(256, FIELDS, 2, LANES)
    x = lax.all_to_all(x, ("rows", "cols"), split_axis=0, concat_axis=0, tiled=True)
    return x.reshape(1536, LANES)


def shards(signal, kernel, gate_values, grad_out):
    inputs = [flat(x) for x in (signal, kernel, gate_values, grad_out)]
    stored = [pltpu.with_memory_space_constraint(x, pltpu.HBM) for x in inputs]
    done = exchange(run_channel(exchange(run_pack(*stored))))
    return tuple(unflat(x) for x in run_unpack(done, *inputs[2:]))


def solution(mesh):
    place = P(None, "cols", "rows", None)
    return jax.shard_map(
        shards, mesh=mesh, in_specs=(place,) * 4, out_specs=(place,) * 4, check_vma=False
    )
```

```python
import functools

import jax
import jax.numpy as jnp
import ml_dtypes
import numpy as np
from jax import lax
from jax.experimental import pallas as pl
from jax.experimental.pallas import tpu as pltpu
from jax.sharding import PartitionSpec as P

LENGTH = 65536
LANES = 128
FIELDS = 3
EXTRA = 768
ROWS = EXTRA + 48
CHUNK = 448
SCALE = 1.0 / (65536.0 * 256.0)
HALF = jnp.bfloat16


def halves(table):
    high = table.astype(np.float32).astype(ml_dtypes.bfloat16)
    low = (table - high.astype(np.float64)).astype(np.float32).astype(ml_dtypes.bfloat16)
    return high, low


def tall(table):
    return np.concatenate(np.split(table, 2, axis=1))


@functools.lru_cache(maxsize=None)
def tables():
    a = np.arange(32)
    fa = np.arange(16)
    angle = 2.0 * np.pi * (fa[:, None] * a[None, :] % 32) / 32.0
    first = np.zeros((144, 128))
    last = np.zeros((128, 128))
    weight = np.where(fa == 0, 1.0, 2.0)[:, None] * SCALE
    for cl in range(4):
        columns = slice(32 * cl, 32 * cl + 32)
        first[16 * cl : 16 * cl + 16, columns] = np.cos(angle)
        first[64 + 16 * cl : 64 + 16 * cl + 16, columns] = -np.sin(angle)
        first[128 + cl, columns] = np.where(a % 2 == 0, 1.0, -1.0)
        last[16 * cl : 16 * cl + 16, columns] = weight * np.cos(angle)
        last[64 + 16 * cl : 64 + 16 * cl + 16, columns] = -weight * np.sin(angle)
        last[64 + 16 * cl, columns] = np.where(a % 2 == 0, SCALE, -SCALE)
    last = last.T.reshape(4, 32, 128)
    last = np.stack([np.kron([1.0, 0.0], last), np.kron([0.0, 1.0], last)]).transpose(2, 0, 1, 3).reshape(256, 256)
    lane = np.arange(128)
    m = 8 * (lane % 16) + 4 * (lane // 64) + (lane // 16) % 4
    g0 = np.arange(128)
    angle = 2.0 * np.pi * (m[:, None] * g0[None, :] % 128) / 128.0
    middle = np.block([[np.cos(angle), -np.sin(angle)], [np.sin(angle), np.cos(angle)]])
    c16 = np.arange(16)
    angle = 2.0 * np.pi * (c16[:, None] * c16[None, :] % 16) / 16.0
    cosine, sine = (np.kron(np.eye(FIELDS), part) for part in (np.cos(angle), np.sin(angle)))
    extra = np.block([[cosine, sine], [-sine, cosine]])
    fa = np.arange(17)
    phase = 2.0 * np.pi * (16 * fa[:, None] * m[None, :] % LENGTH) / LENGTH
    turn_m = np.zeros((2, 24, 128), np.float32)
    turn_m[0, :17] = np.cos(phase)
    turn_m[1, :17] = np.sin(phase)
    phase = c16[:, None, None] * (fa[None, :, None] + 32 * g0[None, None, :]) % LENGTH
    phase = 2.0 * np.pi * phase / LENGTH
    turn_c = np.stack([np.cos(phase), np.sin(phase)]).astype(np.float32)
    turn_x = np.tile(turn_c[:, :, 16], (1, FIELDS, 1))
    turn_c = np.ascontiguousarray(turn_c[:, :, :16])
    return (
        *halves(first), *halves(tall(middle)), *halves(extra), turn_m, turn_c, turn_x, *halves(tall(last))
    )


def split(values):
    high = values.astype(HALF)
    return high, (values - high.astype(jnp.float32)).astype(HALF)


def product(left, right, dims):
    def one(x, y):
        return lax.dot_general(x, y, (dims, ((), ())), preferred_element_type=jnp.float32)

    return one(left[0], right[0]) + (one(left[0], right[1]) + one(left[1], right[0]))


def sixteen(values, sign):
    def add(x, y):
        return (x[0] + y[0], x[1] + y[1])

    def sub(x, y):
        return (x[0] - y[0], x[1] - y[1])

    def quarter(x):
        return (-x[1], x[0]) if sign > 0 else (x[1], -x[0])

    def four(v):
        s, d = add(v[0], v[2]), sub(v[0], v[2])
        t, u = add(v[1], v[3]), quarter(sub(v[1], v[3]))
        return [add(s, t), add(d, u), sub(s, t), sub(d, u)]

    def turned(x, k):
        if k == 0:
            return x
        if k == 4:
            return quarter(x)
        cosine, sine = float(np.cos(np.pi * k / 8)), float(sign * np.sin(np.pi * k / 8))
        return (x[0] * cosine - x[1] * sine, x[0] * sine + x[1] * cosine)

    inner = [four(values[n::4]) for n in range(4)]
    outer = [four([turned(inner[n][k], n * k) for n in range(4)]) for k in range(4)]
    return [outer[k % 4][k // 4] for k in range(16)]


def times(x, y):
    return (x[0] * y[0] - x[1] * y[1], x[0] * y[1] + x[1] * y[0])


def times_conj(x, y):
    return (x[0] * y[0] + x[1] * y[1], x[1] * y[0] - x[0] * y[1])


def pack_kernel(signal, kernel, gate, grad, out):
    for field in range(FIELDS):
        for half in range(2):
            for bl in range(2):
                parts = []
                for cl in range(4):
                    rows = pl.ds(bl * 8 + half * 4 + cl, 32, stride=16)
                    if field == 0:
                        parts.append(signal[rows, :])
                    elif field == 1:
                        parts.append(kernel[rows, :])
                    else:
                        parts.append(gate[rows, :] * grad[rows, :])
                block = jnp.concatenate(parts, axis=0).T
                out[pl.ds(768 * half + field * 2 + bl, 128, stride=6), :] = block


def unpack_kernel(arrived, last_hi, last_lo, gate, grad, gated, signal_grad, kernel_grad, gate_grad):
    last = [jnp.concatenate([ref[0:256, :], ref[256:512, :]], axis=1) for ref in (last_hi, last_lo)]
    for field in range(FIELDS):
        block = [
            [arrived[pl.ds(768 * half + field * 2 + bl, 128, stride=6), :] for half in range(2)]
            for bl in range(2)
        ]
        block = jnp.concatenate([jnp.concatenate(b, axis=1) for b in block], axis=0)
        block = product(last, split(block), ((1,), (1,)))
        for a in range(32):
            for bl in range(2):
                rows = pl.ds(16 * a + 8 * bl, 8)
                part = block[8 * a : 8 * a + 8, 128 * bl : 128 * bl + 128]
                if field == 0:
                    gated[rows, :] = gate[rows, :] * part
                    gate_grad[rows, :] = grad[rows, :] * part
                elif field == 1:
                    signal_grad[rows, :] = part
                else:
                    kernel_grad[rows, :] = part


def channel_kernel(
    arrived, first_hi, first_lo, middle_hi, middle_lo, extra_hi, extra_lo, turn_m, turn_c, turn_x, out, data,
):
    re, im = slice(0, 128), slice(128, 256)
    cos_m, sin_m = turn_m[0, 0:16], turn_m[1, 0:16]
    cos_x, sin_x = turn_m[0, 16:17], turn_m[1, 16:17]
    first = (first_hi[...], first_lo[...])
    for field in range(FIELDS):
        blocks = [
            arrived[pl.ds(field * 2 + bl, 256, stride=6), :].reshape(4, 2, 2, 16, 128) for bl in range(2)
        ]
        for z0 in range(2):
            block = jnp.concatenate([b[:, z0, l].reshape(64, 128) for l in range(2) for b in blocks], axis=0)
            mixed = product(first, split(block), ((1,), (1,)))
            for l in range(2):
                lanes = slice(128 * l, 128 * l + 128)
                for cl in range(4):
                    rows = pl.ds(48 * (8 * z0 + 4 * l + cl) + 16 * field, 16)
                    x, y = mixed[16 * cl : 16 * cl + 16, lanes], mixed[64 + 16 * cl : 80 + 16 * cl, lanes]
                    data[rows, re] = x * cos_m + y * sin_m
                    data[rows, im] = y * cos_m - x * sin_m
                rows = pl.ds(EXTRA + 16 * field + 8 * z0 + 4 * l, 4)
                x = mixed[128:132, lanes]
                data[rows, re] = x * cos_x
                data[rows, im] = -(x * sin_x)

    middle = [jnp.concatenate([ref[0:256, :], ref[256:512, :]], axis=1) for ref in (middle_hi, middle_lo)]

    def along_lanes(dims):
        for start in range(0, ROWS, CHUNK):
            rows = pl.ds(start, min(CHUNK, ROWS - start))
            data[rows, :] = product(split(data[rows, :]), middle, dims)

    def multiply(spectra):
        signal, kernel, grad = spectra
        return (
            [times(s, k) for s, k in zip(signal, kernel)],
            [times_conj(g, k) for g, k in zip(grad, kernel)],
            [times_conj(g, s) for g, s in zip(grad, signal)],
        )

    along_lanes(((1,), (0,)))
    for start in (0, 8):
        turn = [(turn_c[0, c, start : start + 8], turn_c[1, c, start : start + 8]) for c in range(16)]
        spectra = []
        for field in range(FIELDS):
            rows = [pl.ds(start + 16 * field + 48 * c, 8) for c in range(16)]
            values = [times_conj((data[r, re], data[r, im]), t) for r, t in zip(rows, turn)]
            spectra.append(sixteen(values, -1))
        for field, result in enumerate(multiply(spectra)):
            for c, (v, t) in enumerate(zip(sixteen(result, 1), turn)):
                rows = pl.ds(start + 16 * field + 48 * c, 8)
                data[rows, re], data[rows, im] = times(v, t)
    rows, turn = pl.ds(EXTRA, 48), (turn_x[0], turn_x[1])
    extra = (extra_hi[...], extra_lo[...])
    values = jnp.concatenate(times_conj((data[rows, re], data[rows, im]), turn), axis=0)
    values = product(extra, split(values), ((1,), (0,)))
    spectra = [[(values[16 * f : 16 * f + 16], values[48 + 16 * f : 64 + 16 * f])] for f in range(FIELDS)]
    results = multiply(spectra)
    values = jnp.concatenate([result[0][part] for part in range(2) for result in results], axis=0)
    values = product(extra, split(values), ((0,), (0,)))
    data[rows, re], data[rows, im] = times((values[:48], values[48:]), turn)
    along_lanes(((1,), (1,)))

    lead = lax.broadcasted_iota(jnp.int32, (16, 128), 0) == 0
    for field in range(FIELDS):
        done = []
        for z0 in range(2):
            for l in range(2):
                rows = pl.ds(EXTRA + 16 * field + 8 * z0 + 4 * l, 4)
                extra = data[rows, re] * cos_x - data[rows, im] * sin_x
                reals, imags = [], []
                for cl in range(4):
                    rows = pl.ds(48 * (8 * z0 + 4 * l + cl) + 16 * field, 16)
                    x, y = data[rows, re], data[rows, im]
                    reals.append(x * cos_m - y * sin_m)
                    imags.append(jnp.where(lead, extra[cl : cl + 1], y * cos_m + x * sin_m))
                done.append(jnp.concatenate(reals + imags, axis=0).T)
        for bl in range(2):
            parts = [d[64 * bl : 64 * bl + 64].reshape(4, 1, 16, 128) for d in done]
            block = jnp.concatenate(parts, axis=1).reshape(256, 128)
            out[pl.ds(field * 2 + bl, 256, stride=6), :] = block


VMEM = pl.BlockSpec(memory_space=pltpu.VMEM)


def call(body, operands, in_specs, shapes, out_specs, scratch=(), limit=24 << 20):
    return pl.pallas_call(
        body,
        out_shape=shapes,
        in_specs=in_specs,
        out_specs=out_specs,
        scratch_shapes=scratch,
        compiler_params=pltpu.CompilerParams(vmem_limit_bytes=limit),
    )(*operands)


WIDE = jax.ShapeDtypeStruct((1536, LANES), jnp.float32)
OWN = jax.ShapeDtypeStruct((512, LANES), jnp.float32)


def run_pack(signal, kernel, gate, grad):
    return call(pack_kernel, (signal, kernel, gate, grad), [VMEM] * 4, WIDE, VMEM)


def run_channel(arrived):
    constants = tables()[:-2]
    scratch = [pltpu.VMEM((ROWS, 256), jnp.float32)]
    specs = [VMEM] * (1 + len(constants))
    return call(channel_kernel, (arrived, *constants), specs, WIDE, VMEM, scratch)


def run_unpack(arrived, gate, grad):
    operands = (arrived, *tables()[-2:], gate, grad)
    return call(unpack_kernel, operands, [VMEM] * 5, (OWN,) * 4, (VMEM,) * 4)


def flat(x):
    return x.reshape(32, 2, 4, 2, LANES).transpose(0, 1, 3, 2, 4).reshape(512, LANES)


def unflat(x):
    return x.reshape(32, 2, 2, 4, LANES).transpose(0, 1, 3, 2, 4).reshape(32, 2, 4, 256)


def exchange(x):
    x = x.reshape(256, FIELDS, 2, LANES)
    x = lax.all_to_all(x, ("rows", "cols"), split_axis=0, concat_axis=0, tiled=True)
    return x.reshape(1536, LANES)


def shards(signal, kernel, gate_values, grad_out):
    inputs = [flat(x) for x in (signal, kernel, gate_values, grad_out)]
    stored = [pltpu.with_memory_space_constraint(x, pltpu.HBM) for x in inputs]
    done = exchange(run_channel(exchange(run_pack(*stored))))
    return tuple(unflat(x) for x in run_unpack(done, *inputs[2:]))


def solution(mesh):
    place = P(None, "cols", "rows", None)
    return jax.shard_map(
        shards, mesh=mesh, in_specs=(place,) * 4, out_specs=(place,) * 4, check_vma=False
    )
```

```python
import functools

import jax
import jax.numpy as jnp
import ml_dtypes
import numpy as np
from jax import lax
from jax.experimental import pallas as pl
from jax.experimental.pallas import tpu as pltpu
from jax.sharding import PartitionSpec as P

LENGTH = 65536
LISTED = [
    (2 * z + l) * 16 + 8 * h + 2 * x + core
    for z in range(8)
    for core in range(2)
    for x in range(4)
    for h in range(2)
    for l in range(2)
]
LANES = 128
FIELDS = 3
EXTRA = 768
ROWS = EXTRA + 48
CHUNK = 448
SCALE = 1.0 / (65536.0 * 256.0)
HALF = jnp.bfloat16


def halves(table):
    high = table.astype(np.float32).astype(ml_dtypes.bfloat16)
    low = (table - high.astype(np.float64)).astype(np.float32).astype(ml_dtypes.bfloat16)
    return high, low


def tall(table):
    return np.concatenate(np.split(table, 2, axis=1))


@functools.lru_cache(maxsize=None)
def tables():
    a = np.arange(32)
    fa = np.arange(16)
    angle = 2.0 * np.pi * (fa[:, None] * a[None, :] % 32) / 32.0
    first = np.zeros((144, 128))
    last = np.zeros((128, 128))
    weight = np.where(fa == 0, 1.0, 2.0)[:, None] * SCALE
    for cl in range(4):
        columns = slice(32 * cl, 32 * cl + 32)
        first[16 * cl : 16 * cl + 16, columns] = np.cos(angle)
        first[64 + 16 * cl : 64 + 16 * cl + 16, columns] = -np.sin(angle)
        first[128 + cl, columns] = np.where(a % 2 == 0, 1.0, -1.0)
        last[16 * cl : 16 * cl + 16, columns] = weight * np.cos(angle)
        last[64 + 16 * cl : 64 + 16 * cl + 16, columns] = -weight * np.sin(angle)
        last[64 + 16 * cl, columns] = np.where(a % 2 == 0, SCALE, -SCALE)
    last = last.T.reshape(4, 32, 128)
    last = np.stack([np.kron([1.0, 0.0], last), np.kron([0.0, 1.0], last)]).transpose(2, 0, 1, 3).reshape(256, 256)
    first = first.reshape(144, 4, 2, 16).transpose(0, 3, 2, 1).reshape(144, 128)
    lane = np.arange(128)
    q = 8 * (lane % 2) + 2 * (lane // 2 % 4) + lane // 8 % 2
    m = 8 * q + 4 * (lane // 64) + lane // 16 % 4
    g0 = np.arange(128)
    angle = 2.0 * np.pi * (m[:, None] * g0[None, :] % 128) / 128.0
    middle = np.block([[np.cos(angle), -np.sin(angle)], [np.sin(angle), np.cos(angle)]])
    c16 = np.arange(16)
    angle = 2.0 * np.pi * (c16[:, None] * c16[None, :] % 16) / 16.0
    cosine, sine = (np.kron(np.eye(FIELDS), part) for part in (np.cos(angle), np.sin(angle)))
    extra = np.block([[cosine, sine], [-sine, cosine]])
    fa = np.arange(17)
    phase = 2.0 * np.pi * (16 * fa[:, None] * m[None, :] % LENGTH) / LENGTH
    turn_m = np.zeros((2, 24, 128), np.float32)
    turn_m[0, :17] = np.cos(phase)
    turn_m[1, :17] = np.sin(phase)
    phase = c16[:, None, None] * (fa[None, :, None] + 32 * g0[None, None, :]) % LENGTH
    phase = 2.0 * np.pi * phase / LENGTH
    turn_c = np.stack([np.cos(phase), np.sin(phase)]).astype(np.float32)
    turn_x = np.tile(turn_c[:, :, 16], (1, FIELDS, 1))
    turn_c = np.ascontiguousarray(turn_c[:, :, :16])
    return (
        *halves(first), *halves(tall(middle)), *halves(extra), turn_m, turn_c, turn_x, *halves(tall(last))
    )


def split(values):
    high = values.astype(HALF)
    return high, (values - high.astype(jnp.float32)).astype(HALF)


def product(left, right, dims):
    def one(x, y):
        return lax.dot_general(x, y, (dims, ((), ())), preferred_element_type=jnp.float32)

    return one(left[0], right[0]) + (one(left[0], right[1]) + one(left[1], right[0]))


def sixteen(values, sign):
    def add(x, y):
        return (x[0] + y[0], x[1] + y[1])

    def sub(x, y):
        return (x[0] - y[0], x[1] - y[1])

    def quarter(x):
        return (-x[1], x[0]) if sign > 0 else (x[1], -x[0])

    def four(v):
        s, d = add(v[0], v[2]), sub(v[0], v[2])
        t, u = add(v[1], v[3]), quarter(sub(v[1], v[3]))
        return [add(s, t), add(d, u), sub(s, t), sub(d, u)]

    def turned(x, k):
        if k == 0:
            return x
        if k == 4:
            return quarter(x)
        cosine, sine = float(np.cos(np.pi * k / 8)), float(sign * np.sin(np.pi * k / 8))
        return (x[0] * cosine - x[1] * sine, x[0] * sine + x[1] * cosine)

    inner = [four(values[n::4]) for n in range(4)]
    outer = [four([turned(inner[n][k], n * k) for n in range(4)]) for k in range(4)]
    return [outer[k % 4][k // 4] for k in range(16)]


def times(x, y):
    return (x[0] * y[0] - x[1] * y[1], x[0] * y[1] + x[1] * y[0])


def times_conj(x, y):
    return (x[0] * y[0] + x[1] * y[1], x[1] * y[0] - x[0] * y[1])


def pack_kernel(signal, kernel, gate, grad, out):
    for field in range(FIELDS):
        block = signal[...] if field == 0 else kernel[...] if field == 1 else gate[...] * grad[...]
        block = block.reshape(2, 16, 2, 8, 128)
        for half in range(2):
            for bl in range(2):
                parts = [block[k, :, bl, 4 * half : 4 * half + 4] for k in range(2)]
                part = jnp.concatenate(parts, axis=1).reshape(128, 128)
                out[pl.ds(768 * half + field * 2 + bl, 128, stride=6), :] = part.T


def unpack_kernel(arrived, last_hi, last_lo, gate, grad, gated, signal_grad, kernel_grad, gate_grad):
    last = [jnp.concatenate([ref[0:256, :], ref[256:512, :]], axis=1) for ref in (last_hi, last_lo)]
    for field in range(FIELDS):
        block = [
            [arrived[pl.ds(768 * half + field * 2 + bl, 128, stride=6), :] for half in range(2)]
            for bl in range(2)
        ]
        block = jnp.concatenate([jnp.concatenate(b, axis=1) for b in block], axis=0)
        block = product(last, split(block), ((1,), (1,)))
        for a in range(32):
            for bl in range(2):
                rows = pl.ds(16 * a + 8 * bl, 8)
                part = block[8 * a : 8 * a + 8, 128 * bl : 128 * bl + 128]
                if field == 0:
                    gated[rows, :] = gate[rows, :] * part
                    gate_grad[rows, :] = grad[rows, :] * part
                elif field == 1:
                    signal_grad[rows, :] = part
                else:
                    kernel_grad[rows, :] = part


def channel_kernel(
    arrived, first_hi, first_lo, middle_hi, middle_lo, extra_hi, extra_lo, turn_m, turn_c, turn_x, out, data,
):
    re, im = slice(0, 128), slice(128, 256)
    cos_m, sin_m = turn_m[0, 0:16], turn_m[1, 0:16]
    cos_x, sin_x = turn_m[0, 16:17], turn_m[1, 16:17]
    first = (first_hi[...], first_lo[...])
    for field in range(FIELDS):
        blocks = [
            arrived[pl.ds(6 * l + field * 2 + bl, 128, stride=12), :].reshape(4, 2, 16, 128)
            for l in range(2)
            for bl in range(2)
        ]
        for z0 in range(2):
            block = jnp.concatenate([b[:, z0].reshape(64, 128) for b in blocks], axis=0)
            mixed = product(first, split(block), ((1,), (1,)))
            for l in range(2):
                lanes = slice(128 * l, 128 * l + 128)
                for cl in range(4):
                    rows = pl.ds(48 * (8 * z0 + 4 * l + cl) + 16 * field, 16)
                    x, y = mixed[16 * cl : 16 * cl + 16, lanes], mixed[64 + 16 * cl : 80 + 16 * cl, lanes]
                    data[rows, re] = x * cos_m + y * sin_m
                    data[rows, im] = y * cos_m - x * sin_m
                rows = pl.ds(EXTRA + 16 * field + 8 * z0 + 4 * l, 4)
                x = mixed[128:132, lanes]
                data[rows, re] = x * cos_x
                data[rows, im] = -(x * sin_x)

    middle = [jnp.concatenate([ref[0:256, :], ref[256:512, :]], axis=1) for ref in (middle_hi, middle_lo)]

    def along_lanes(dims):
        for start in range(0, ROWS, CHUNK):
            rows = pl.ds(start, min(CHUNK, ROWS - start))
            data[rows, :] = product(split(data[rows, :]), middle, dims)

    def multiply(spectra):
        signal, kernel, grad = spectra
        return (
            [times(s, k) for s, k in zip(signal, kernel)],
            [times_conj(g, k) for g, k in zip(grad, kernel)],
            [times_conj(g, s) for g, s in zip(grad, signal)],
        )

    along_lanes(((1,), (0,)))
    for start in (0, 8):
        turn = [(turn_c[0, c, start : start + 8], turn_c[1, c, start : start + 8]) for c in range(16)]
        spectra = []
        for field in range(FIELDS):
            rows = [pl.ds(start + 16 * field + 48 * c, 8) for c in range(16)]
            values = [times_conj((data[r, re], data[r, im]), t) for r, t in zip(rows, turn)]
            spectra.append(sixteen(values, -1))
        for field, result in enumerate(multiply(spectra)):
            for c, (v, t) in enumerate(zip(sixteen(result, 1), turn)):
                rows = pl.ds(start + 16 * field + 48 * c, 8)
                data[rows, re], data[rows, im] = times(v, t)
    rows, turn = pl.ds(EXTRA, 48), (turn_x[0], turn_x[1])
    extra = (extra_hi[...], extra_lo[...])
    values = jnp.concatenate(times_conj((data[rows, re], data[rows, im]), turn), axis=0)
    values = product(extra, split(values), ((1,), (0,)))
    spectra = [[(values[16 * f : 16 * f + 16], values[48 + 16 * f : 64 + 16 * f])] for f in range(FIELDS)]
    results = multiply(spectra)
    values = jnp.concatenate([result[0][part] for part in range(2) for result in results], axis=0)
    values = product(extra, split(values), ((0,), (0,)))
    data[rows, re], data[rows, im] = times((values[:48], values[48:]), turn)
    along_lanes(((1,), (1,)))

    lead = lax.broadcasted_iota(jnp.int32, (16, 128), 0) == 0
    for field in range(FIELDS):
        done = []
        for z0 in range(2):
            for l in range(2):
                rows = pl.ds(EXTRA + 16 * field + 8 * z0 + 4 * l, 4)
                extra = data[rows, re] * cos_x - data[rows, im] * sin_x
                reals, imags = [], []
                for cl in range(4):
                    rows = pl.ds(48 * (8 * z0 + 4 * l + cl) + 16 * field, 16)
                    x, y = data[rows, re], data[rows, im]
                    reals.append(x * cos_m - y * sin_m)
                    imags.append(jnp.where(lead, extra[cl : cl + 1], y * cos_m + x * sin_m))
                done.append(jnp.concatenate(reals + imags, axis=0).T)
        for l in range(2):
            for bl in range(2):
                parts = [d[64 * bl : 64 * bl + 64].reshape(4, 1, 16, 128) for d in done[l::2]]
                block = jnp.concatenate(parts, axis=1).reshape(128, 128)
                out[pl.ds(6 * l + field * 2 + bl, 128, stride=12), :] = block


VMEM = pl.BlockSpec(memory_space=pltpu.VMEM)


def call(body, operands, in_specs, shapes, out_specs, scratch=(), limit=24 << 20):
    return pl.pallas_call(
        body,
        out_shape=shapes,
        in_specs=in_specs,
        out_specs=out_specs,
        scratch_shapes=scratch,
        compiler_params=pltpu.CompilerParams(vmem_limit_bytes=limit),
    )(*operands)


WIDE = jax.ShapeDtypeStruct((1536, LANES), jnp.float32)
OWN = jax.ShapeDtypeStruct((512, LANES), jnp.float32)


def run_pack(signal, kernel, gate, grad):
    return call(pack_kernel, (signal, kernel, gate, grad), [VMEM] * 4, WIDE, VMEM)


def run_channel(arrived):
    constants = tables()[:-2]
    scratch = [pltpu.VMEM((ROWS, 256), jnp.float32)]
    specs = [VMEM] * (1 + len(constants))
    return call(channel_kernel, (arrived, *constants), specs, WIDE, VMEM, scratch)


def run_unpack(arrived, gate, grad):
    operands = (arrived, *tables()[-2:], gate, grad)
    return call(unpack_kernel, operands, [VMEM] * 5, (OWN,) * 4, (VMEM,) * 4)


def flat(x):
    return x.reshape(32, 2, 4, 2, LANES).transpose(0, 1, 3, 2, 4).reshape(512, LANES)


def unflat(x):
    return x.reshape(32, 2, 2, 4, LANES).transpose(0, 1, 3, 2, 4).reshape(32, 2, 4, 256)


def exchange(x):
    x = x.reshape(256, FIELDS, 2, LANES)
    x = lax.all_to_all(
        x, ("rows", "cols"), split_axis=0, concat_axis=0, tiled=True, axis_index_groups=[LISTED]
    )
    return x.reshape(1536, LANES)


def shards(signal, kernel, gate_values, grad_out):
    inputs = [flat(x) for x in (signal, kernel, gate_values, grad_out)]
    stored = [pltpu.with_memory_space_constraint(x, pltpu.HBM) for x in inputs]
    done = exchange(run_channel(exchange(run_pack(*stored))))
    return tuple(unflat(x) for x in run_unpack(done, *inputs[2:]))


def solution(mesh):
    place = P(None, "cols", "rows", None)
    return jax.shard_map(
        shards, mesh=mesh, in_specs=(place,) * 4, out_specs=(place,) * 4, check_vma=False
    )
```

```python
import functools

import jax
import jax.numpy as jnp
import ml_dtypes
import numpy as np
from jax import lax
from jax.experimental import pallas as pl
from jax.experimental.pallas import tpu as pltpu
from jax.sharding import PartitionSpec as P

LENGTH = 65536
LISTED = [
    (2 * z + l) * 16 + 8 * h + 2 * x + core
    for z in range(8)
    for core in range(2)
    for x in range(4)
    for h in range(2)
    for l in range(2)
]
LANES = 128
FIELDS = 3
EXTRA = 768
ROWS = EXTRA + 48
CHUNK = 448
SCALE = 1.0 / (65536.0 * 256.0)
HALF = jnp.bfloat16


def halves(table):
    high = table.astype(np.float32).astype(ml_dtypes.bfloat16)
    low = (table - high.astype(np.float64)).astype(np.float32).astype(ml_dtypes.bfloat16)
    return high, low


def tall(table):
    return np.concatenate(np.split(table, 2, axis=1))


@functools.lru_cache(maxsize=None)
def tables():
    a = np.arange(32)
    fa = np.arange(16)
    angle = 2.0 * np.pi * (fa[:, None] * a[None, :] % 32) / 32.0
    first = np.zeros((144, 128))
    last = np.zeros((128, 128))
    weight = np.where(fa == 0, 1.0, 2.0)[:, None] * SCALE
    for cl in range(4):
        columns = slice(32 * cl, 32 * cl + 32)
        first[16 * cl : 16 * cl + 16, columns] = np.cos(angle)
        first[64 + 16 * cl : 64 + 16 * cl + 16, columns] = -np.sin(angle)
        first[128 + cl, columns] = np.where(a % 2 == 0, 1.0, -1.0)
        last[16 * cl : 16 * cl + 16, columns] = weight * np.cos(angle)
        last[64 + 16 * cl : 64 + 16 * cl + 16, columns] = -weight * np.sin(angle)
        last[64 + 16 * cl, columns] = np.where(a % 2 == 0, SCALE, -SCALE)
    last = last.T.reshape(4, 32, 128)
    last = np.stack([np.kron([1.0, 0.0], last), np.kron([0.0, 1.0], last)]).transpose(2, 0, 1, 3).reshape(256, 256)
    first = first.reshape(144, 4, 2, 16).transpose(0, 3, 2, 1).reshape(144, 128)
    lane = np.arange(128)
    q = 8 * (lane % 2) + 2 * (lane // 2 % 4) + lane // 8 % 2
    m = 8 * q + 4 * (lane // 64) + lane // 16 % 4
    g0 = np.arange(128)
    angle = 2.0 * np.pi * (m[:, None] * g0[None, :] % 128) / 128.0
    middle = np.block([[np.cos(angle), -np.sin(angle)], [np.sin(angle), np.cos(angle)]])
    c16 = np.arange(16)
    angle = 2.0 * np.pi * (c16[:, None] * c16[None, :] % 16) / 16.0
    cosine, sine = (np.kron(np.eye(FIELDS), part) for part in (np.cos(angle), np.sin(angle)))
    extra = np.block([[cosine, sine], [-sine, cosine]])
    fa = np.arange(17)
    phase = 2.0 * np.pi * (16 * fa[:, None] * m[None, :] % LENGTH) / LENGTH
    turn_m = np.zeros((2, 24, 128), np.float32)
    turn_m[0, :17] = np.cos(phase)
    turn_m[1, :17] = np.sin(phase)
    phase = c16[:, None, None] * (fa[None, :, None] + 32 * g0[None, None, :]) % LENGTH
    phase = 2.0 * np.pi * phase / LENGTH
    turn_c = np.stack([np.cos(phase), np.sin(phase)]).astype(np.float32)
    turn_x = np.tile(turn_c[:, :, 16], (1, FIELDS, 1))
    turn_c = np.ascontiguousarray(turn_c[:, :, :16])
    return (
        *halves(first), *halves(tall(middle)), *halves(tall(middle.T)), *halves(extra), *halves(extra.T), turn_m, turn_c, turn_x, *halves(tall(last))
    )


def split(values):
    high = values.astype(HALF)
    return high, (values - high.astype(jnp.float32)).astype(HALF)


def product(left, right, dims):
    def one(x, y):
        return lax.dot_general(x, y, (dims, ((), ())), preferred_element_type=jnp.float32)

    return one(left[0], right[0]) + (one(left[0], right[1]) + one(left[1], right[0]))


def sixteen(values, sign):
    def add(x, y):
        return (x[0] + y[0], x[1] + y[1])

    def sub(x, y):
        return (x[0] - y[0], x[1] - y[1])

    def quarter(x):
        return (-x[1], x[0]) if sign > 0 else (x[1], -x[0])

    def four(v):
        s, d = add(v[0], v[2]), sub(v[0], v[2])
        t, u = add(v[1], v[3]), quarter(sub(v[1], v[3]))
        return [add(s, t), add(d, u), sub(s, t), sub(d, u)]

    def turned(x, k):
        if k == 0:
            return x
        if k == 4:
            return quarter(x)
        cosine, sine = float(np.cos(np.pi * k / 8)), float(sign * np.sin(np.pi * k / 8))
        return (x[0] * cosine - x[1] * sine, x[0] * sine + x[1] * cosine)

    inner = [four(values[n::4]) for n in range(4)]
    outer = [four([turned(inner[n][k], n * k) for n in range(4)]) for k in range(4)]
    return [outer[k % 4][k // 4] for k in range(16)]


def times(x, y):
    return (x[0] * y[0] - x[1] * y[1], x[0] * y[1] + x[1] * y[0])


def times_conj(x, y):
    return (x[0] * y[0] + x[1] * y[1], x[1] * y[0] - x[0] * y[1])


def pack_kernel(signal, kernel, gate, grad, out):
    for field in range(FIELDS):
        block = signal[...] if field == 0 else kernel[...] if field == 1 else gate[...] * grad[...]
        block = block.reshape(2, 16, 2, 8, 128)
        for half in range(2):
            for bl in range(2):
                parts = [block[k, :, bl, 4 * half : 4 * half + 4] for k in range(2)]
                part = jnp.concatenate(parts, axis=1).reshape(128, 128)
                out[pl.ds(768 * half + field * 2 + bl, 128, stride=6), :] = part.T


def unpack_kernel(arrived, last_hi, last_lo, gate, grad, gated, signal_grad, kernel_grad, gate_grad):
    last = [jnp.concatenate([ref[0:256, :], ref[256:512, :]], axis=1) for ref in (last_hi, last_lo)]
    for field in range(FIELDS):
        block = [
            [arrived[pl.ds(768 * half + field * 2 + bl, 128, stride=6), :] for half in range(2)]
            for bl in range(2)
        ]
        block = jnp.concatenate([jnp.concatenate(b, axis=1) for b in block], axis=0)
        block = product(last, split(block), ((1,), (1,)))
        for a in range(32):
            for bl in range(2):
                rows = pl.ds(16 * a + 8 * bl, 8)
                part = block[8 * a : 8 * a + 8, 128 * bl : 128 * bl + 128]
                if field == 0:
                    gated[rows, :] = gate[rows, :] * part
                    gate_grad[rows, :] = grad[rows, :] * part
                elif field == 1:
                    signal_grad[rows, :] = part
                else:
                    kernel_grad[rows, :] = part


def channel_kernel(
    arrived, first_hi, first_lo, middle_hi, middle_lo, inverse_hi, inverse_lo, extra_hi, extra_lo, back_hi, back_lo, turn_m, turn_c, turn_x,
    out, data,
):
    re, im = slice(0, 128), slice(128, 256)
    cos_m, sin_m = turn_m[0, 0:16], turn_m[1, 0:16]
    cos_x, sin_x = turn_m[0, 16:17], turn_m[1, 16:17]
    first = (first_hi[...], first_lo[...])
    for field in range(FIELDS):
        blocks = [
            arrived[pl.ds(6 * l + field * 2 + bl, 128, stride=12), :].reshape(4, 2, 16, 128)
            for l in range(2)
            for bl in range(2)
        ]
        for z0 in range(2):
            block = jnp.concatenate([b[:, z0].reshape(64, 128) for b in blocks], axis=0)
            mixed = product(first, split(block), ((1,), (1,)))
            for l in range(2):
                lanes = slice(128 * l, 128 * l + 128)
                for cl in range(4):
                    rows = pl.ds(48 * (8 * z0 + 4 * l + cl) + 16 * field, 16)
                    x, y = mixed[16 * cl : 16 * cl + 16, lanes], mixed[64 + 16 * cl : 80 + 16 * cl, lanes]
                    data[rows, re] = x * cos_m + y * sin_m
                    data[rows, im] = y * cos_m - x * sin_m
                rows = pl.ds(EXTRA + 16 * field + 8 * z0 + 4 * l, 4)
                x = mixed[128:132, lanes]
                data[rows, re] = x * cos_x
                data[rows, im] = -(x * sin_x)

    def along_lanes(refs):
        table = [jnp.concatenate([ref[0:256, :], ref[256:512, :]], axis=1) for ref in refs]
        for start in range(0, ROWS, CHUNK):
            rows = pl.ds(start, min(CHUNK, ROWS - start))
            data[rows, :] = product(split(data[rows, :]), table, ((1,), (0,)))

    def multiply(spectra):
        signal, kernel, grad = spectra
        return (
            [times(s, k) for s, k in zip(signal, kernel)],
            [times_conj(g, k) for g, k in zip(grad, kernel)],
            [times_conj(g, s) for g, s in zip(grad, signal)],
        )

    along_lanes((middle_hi, middle_lo))
    for start in (0, 8):
        turn = [(turn_c[0, c, start : start + 8], turn_c[1, c, start : start + 8]) for c in range(16)]
        spectra = []
        for field in range(FIELDS):
            rows = [pl.ds(start + 16 * field + 48 * c, 8) for c in range(16)]
            values = [times_conj((data[r, re], data[r, im]), t) for r, t in zip(rows, turn)]
            spectra.append(sixteen(values, -1))
        for field, result in enumerate(multiply(spectra)):
            for c, (v, t) in enumerate(zip(sixteen(result, 1), turn)):
                rows = pl.ds(start + 16 * field + 48 * c, 8)
                data[rows, re], data[rows, im] = times(v, t)
    rows, turn = pl.ds(EXTRA, 48), (turn_x[0], turn_x[1])
    extra = (extra_hi[...], extra_lo[...])
    values = jnp.concatenate(times_conj((data[rows, re], data[rows, im]), turn), axis=0)
    values = product(extra, split(values), ((1,), (0,)))
    spectra = [[(values[16 * f : 16 * f + 16], values[48 + 16 * f : 64 + 16 * f])] for f in range(FIELDS)]
    results = multiply(spectra)
    values = jnp.concatenate([result[0][part] for part in range(2) for result in results], axis=0)
    values = product((back_hi[...], back_lo[...]), split(values), ((1,), (0,)))
    data[rows, re], data[rows, im] = times((values[:48], values[48:]), turn)
    along_lanes((inverse_hi, inverse_lo))

    lead = lax.broadcasted_iota(jnp.int32, (16, 128), 0) == 0
    for field in range(FIELDS):
        done = []
        for z0 in range(2):
            for l in range(2):
                rows = pl.ds(EXTRA + 16 * field + 8 * z0 + 4 * l, 4)
                extra = data[rows, re] * cos_x - data[rows, im] * sin_x
                reals, imags = [], []
                for cl in range(4):
                    rows = pl.ds(48 * (8 * z0 + 4 * l + cl) + 16 * field, 16)
                    x, y = data[rows, re], data[rows, im]
                    reals.append(x * cos_m - y * sin_m)
                    imags.append(jnp.where(lead, extra[cl : cl + 1], y * cos_m + x * sin_m))
                done.append(jnp.concatenate(reals + imags, axis=0).T)
        for l in range(2):
            for bl in range(2):
                parts = [d[64 * bl : 64 * bl + 64].reshape(4, 1, 16, 128) for d in done[l::2]]
                block = jnp.concatenate(parts, axis=1).reshape(128, 128)
                out[pl.ds(6 * l + field * 2 + bl, 128, stride=12), :] = block


VMEM = pl.BlockSpec(memory_space=pltpu.VMEM)


def call(body, operands, in_specs, shapes, out_specs, scratch=(), limit=24 << 20):
    return pl.pallas_call(
        body,
        out_shape=shapes,
        in_specs=in_specs,
        out_specs=out_specs,
        scratch_shapes=scratch,
        compiler_params=pltpu.CompilerParams(vmem_limit_bytes=limit),
    )(*operands)


WIDE = jax.ShapeDtypeStruct((1536, LANES), jnp.float32)
OWN = jax.ShapeDtypeStruct((512, LANES), jnp.float32)


def run_pack(signal, kernel, gate, grad):
    return call(pack_kernel, (signal, kernel, gate, grad), [VMEM] * 4, WIDE, VMEM)


def run_channel(arrived):
    constants = tables()[:-2]
    scratch = [pltpu.VMEM((ROWS, 256), jnp.float32)]
    specs = [VMEM] * (1 + len(constants))
    return call(channel_kernel, (arrived, *constants), specs, WIDE, VMEM, scratch)


def run_unpack(arrived, gate, grad):
    operands = (arrived, *tables()[-2:], gate, grad)
    return call(unpack_kernel, operands, [VMEM] * 5, (OWN,) * 4, (VMEM,) * 4)


def flat(x):
    return x.reshape(32, 2, 4, 2, LANES).transpose(0, 1, 3, 2, 4).reshape(512, LANES)


def unflat(x):
    return x.reshape(32, 2, 2, 4, LANES).transpose(0, 1, 3, 2, 4).reshape(32, 2, 4, 256)


def exchange(x):
    x = x.reshape(256, FIELDS, 2, LANES)
    x = lax.all_to_all(
        x, ("rows", "cols"), split_axis=0, concat_axis=0, tiled=True, axis_index_groups=[LISTED]
    )
    return x.reshape(1536, LANES)


def shards(signal, kernel, gate_values, grad_out):
    inputs = [flat(x) for x in (signal, kernel, gate_values, grad_out)]
    stored = [pltpu.with_memory_space_constraint(x, pltpu.HBM) for x in inputs]
    done = exchange(run_channel(exchange(run_pack(*stored))))
    return tuple(unflat(x) for x in run_unpack(done, *inputs[2:]))


def solution(mesh):
    place = P(None, "cols", "rows", None)
    return jax.shard_map(
        shards, mesh=mesh, in_specs=(place,) * 4, out_specs=(place,) * 4, check_vma=False
    )
```

```python
import functools

import jax
import jax.numpy as jnp
import ml_dtypes
import numpy as np
from jax import lax
from jax.experimental import pallas as pl
from jax.experimental.pallas import tpu as pltpu
from jax.sharding import PartitionSpec as P

LENGTH = 65536
LISTED = [
    (2 * z + l) * 16 + 8 * h + 2 * x + core
    for h in range(2)
    for z in range(8)
    for core in range(2)
    for x in range(4)
    for l in range(2)
]
LANES = 128
FIELDS = 3
EXTRA = 768
ROWS = EXTRA + 48
CHUNK = 448
SCALE = 1.0 / (65536.0 * 256.0)
HALF = jnp.bfloat16


def halves(table):
    high = table.astype(np.float32).astype(ml_dtypes.bfloat16)
    low = (table - high.astype(np.float64)).astype(np.float32).astype(ml_dtypes.bfloat16)
    return high, low


def tall(table):
    return np.concatenate(np.split(table, 2, axis=1))


@functools.lru_cache(maxsize=None)
def tables():
    a = np.arange(32)
    fa = np.arange(16)
    angle = 2.0 * np.pi * (fa[:, None] * a[None, :] % 32) / 32.0
    first = np.zeros((144, 128))
    last = np.zeros((128, 128))
    weight = np.where(fa == 0, 1.0, 2.0)[:, None] * SCALE
    for cl in range(4):
        columns = slice(32 * cl, 32 * cl + 32)
        first[16 * cl : 16 * cl + 16, columns] = np.cos(angle)
        first[64 + 16 * cl : 64 + 16 * cl + 16, columns] = -np.sin(angle)
        first[128 + cl, columns] = np.where(a % 2 == 0, 1.0, -1.0)
        last[16 * cl : 16 * cl + 16, columns] = weight * np.cos(angle)
        last[64 + 16 * cl : 64 + 16 * cl + 16, columns] = -weight * np.sin(angle)
        last[64 + 16 * cl, columns] = np.where(a % 2 == 0, SCALE, -SCALE)
    last = last.T.reshape(4, 32, 128)
    last = np.stack([np.kron([1.0, 0.0], last), np.kron([0.0, 1.0], last)]).transpose(2, 0, 1, 3).reshape(256, 256)
    first = first.reshape(144, 4, 2, 16).transpose(0, 3, 2, 1).reshape(144, 128)
    lane = np.arange(128)
    q = 8 * (lane // 32 % 2) + 2 * (lane % 4) + lane // 4 % 2
    m = 8 * q + 4 * (lane // 64) + lane // 8 % 4
    g0 = np.arange(128)
    angle = 2.0 * np.pi * (m[:, None] * g0[None, :] % 128) / 128.0
    middle = np.block([[np.cos(angle), -np.sin(angle)], [np.sin(angle), np.cos(angle)]])
    c16 = np.arange(16)
    angle = 2.0 * np.pi * (c16[:, None] * c16[None, :] % 16) / 16.0
    cosine, sine = (np.kron(np.eye(FIELDS), part) for part in (np.cos(angle), np.sin(angle)))
    extra = np.block([[cosine, sine], [-sine, cosine]])
    fa = np.arange(17)
    phase = 2.0 * np.pi * (16 * fa[:, None] * m[None, :] % LENGTH) / LENGTH
    turn_m = np.zeros((2, 24, 128), np.float32)
    turn_m[0, :17] = np.cos(phase)
    turn_m[1, :17] = np.sin(phase)
    phase = c16[:, None, None] * (fa[None, :, None] + 32 * g0[None, None, :]) % LENGTH
    phase = 2.0 * np.pi * phase / LENGTH
    turn_c = np.stack([np.cos(phase), np.sin(phase)]).astype(np.float32)
    turn_x = np.tile(turn_c[:, :, 16], (1, FIELDS, 1))
    turn_c = np.ascontiguousarray(turn_c[:, :, :16])
    return (
        *halves(first), *halves(tall(middle)), *halves(tall(middle.T)), *halves(extra), *halves(extra.T), turn_m, turn_c, turn_x, *halves(tall(last))
    )


def split(values):
    high = values.astype(HALF)
    return high, (values - high.astype(jnp.float32)).astype(HALF)


def product(left, right, dims):
    def one(x, y):
        return lax.dot_general(x, y, (dims, ((), ())), preferred_element_type=jnp.float32)

    return one(left[0], right[0]) + (one(left[0], right[1]) + one(left[1], right[0]))


def sixteen(values, sign):
    def add(x, y):
        return (x[0] + y[0], x[1] + y[1])

    def sub(x, y):
        return (x[0] - y[0], x[1] - y[1])

    def quarter(x):
        return (-x[1], x[0]) if sign > 0 else (x[1], -x[0])

    def four(v):
        s, d = add(v[0], v[2]), sub(v[0], v[2])
        t, u = add(v[1], v[3]), quarter(sub(v[1], v[3]))
        return [add(s, t), add(d, u), sub(s, t), sub(d, u)]

    def turned(x, k):
        if k == 0:
            return x
        if k == 4:
            return quarter(x)
        cosine, sine = float(np.cos(np.pi * k / 8)), float(sign * np.sin(np.pi * k / 8))
        return (x[0] * cosine - x[1] * sine, x[0] * sine + x[1] * cosine)

    inner = [four(values[n::4]) for n in range(4)]
    outer = [four([turned(inner[n][k], n * k) for n in range(4)]) for k in range(4)]
    return [outer[k % 4][k // 4] for k in range(16)]


def times(x, y):
    return (x[0] * y[0] - x[1] * y[1], x[0] * y[1] + x[1] * y[0])


def times_conj(x, y):
    return (x[0] * y[0] + x[1] * y[1], x[1] * y[0] - x[0] * y[1])


def pack_kernel(signal, kernel, gate, grad, out):
    for field in range(FIELDS):
        block = signal[...] if field == 0 else kernel[...] if field == 1 else gate[...] * grad[...]
        block = block.reshape(2, 16, 2, 8, 128)
        for half in range(2):
            for bl in range(2):
                parts = [block[k, :, bl, 4 * half : 4 * half + 4] for k in range(2)]
                part = jnp.concatenate(parts, axis=1).reshape(128, 128)
                out[pl.ds(768 * half + field * 2 + bl, 128, stride=6), :] = part.T


def unpack_kernel(arrived, last_hi, last_lo, gate, grad, gated, signal_grad, kernel_grad, gate_grad):
    last = [jnp.concatenate([ref[0:256, :], ref[256:512, :]], axis=1) for ref in (last_hi, last_lo)]
    for field in range(FIELDS):
        block = [
            [arrived[pl.ds(768 * half + field * 2 + bl, 128, stride=6), :] for half in range(2)]
            for bl in range(2)
        ]
        block = jnp.concatenate([jnp.concatenate(b, axis=1) for b in block], axis=0)
        block = product(last, split(block), ((1,), (1,)))
        for a in range(32):
            for bl in range(2):
                rows = pl.ds(16 * a + 8 * bl, 8)
                part = block[8 * a : 8 * a + 8, 128 * bl : 128 * bl + 128]
                if field == 0:
                    gated[rows, :] = gate[rows, :] * part
                    gate_grad[rows, :] = grad[rows, :] * part
                elif field == 1:
                    signal_grad[rows, :] = part
                else:
                    kernel_grad[rows, :] = part


def channel_kernel(
    arrived, first_hi, first_lo, middle_hi, middle_lo, inverse_hi, inverse_lo, extra_hi, extra_lo, back_hi, back_lo, turn_m, turn_c, turn_x,
    out, data,
):
    re, im = slice(0, 128), slice(128, 256)
    cos_m, sin_m = turn_m[0, 0:16], turn_m[1, 0:16]
    cos_x, sin_x = turn_m[0, 16:17], turn_m[1, 16:17]
    first = (first_hi[...], first_lo[...])
    for field in range(FIELDS):
        blocks = [
            arrived[pl.ds(6 * l + field * 2 + bl, 128, stride=12), :].reshape(8, 2, 8, 128)
            for l in range(2)
            for bl in range(2)
        ]
        for z0 in range(2):
            block = jnp.concatenate([b[:, z0].reshape(64, 128) for b in blocks], axis=0)
            mixed = product(first, split(block), ((1,), (1,)))
            for l in range(2):
                lanes = slice(128 * l, 128 * l + 128)
                for cl in range(4):
                    rows = pl.ds(48 * (8 * z0 + 4 * l + cl) + 16 * field, 16)
                    x, y = mixed[16 * cl : 16 * cl + 16, lanes], mixed[64 + 16 * cl : 80 + 16 * cl, lanes]
                    data[rows, re] = x * cos_m + y * sin_m
                    data[rows, im] = y * cos_m - x * sin_m
                rows = pl.ds(EXTRA + 16 * field + 8 * z0 + 4 * l, 4)
                x = mixed[128:132, lanes]
                data[rows, re] = x * cos_x
                data[rows, im] = -(x * sin_x)

    def along_lanes(refs):
        table = [jnp.concatenate([ref[0:256, :], ref[256:512, :]], axis=1) for ref in refs]
        for start in range(0, ROWS, CHUNK):
            rows = pl.ds(start, min(CHUNK, ROWS - start))
            data[rows, :] = product(split(data[rows, :]), table, ((1,), (0,)))

    def multiply(spectra):
        signal, kernel, grad = spectra
        return (
            [times(s, k) for s, k in zip(signal, kernel)],
            [times_conj(g, k) for g, k in zip(grad, kernel)],
            [times_conj(g, s) for g, s in zip(grad, signal)],
        )

    along_lanes((middle_hi, middle_lo))
    for start in (0, 8):
        turn = [(turn_c[0, c, start : start + 8], turn_c[1, c, start : start + 8]) for c in range(16)]
        spectra = []
        for field in range(FIELDS):
            rows = [pl.ds(start + 16 * field + 48 * c, 8) for c in range(16)]
            values = [times_conj((data[r, re], data[r, im]), t) for r, t in zip(rows, turn)]
            spectra.append(sixteen(values, -1))
        for field, result in enumerate(multiply(spectra)):
            for c, (v, t) in enumerate(zip(sixteen(result, 1), turn)):
                rows = pl.ds(start + 16 * field + 48 * c, 8)
                data[rows, re], data[rows, im] = times(v, t)
    rows, turn = pl.ds(EXTRA, 48), (turn_x[0], turn_x[1])
    extra = (extra_hi[...], extra_lo[...])
    values = jnp.concatenate(times_conj((data[rows, re], data[rows, im]), turn), axis=0)
    values = product(extra, split(values), ((1,), (0,)))
    spectra = [[(values[16 * f : 16 * f + 16], values[48 + 16 * f : 64 + 16 * f])] for f in range(FIELDS)]
    results = multiply(spectra)
    values = jnp.concatenate([result[0][part] for part in range(2) for result in results], axis=0)
    values = product((back_hi[...], back_lo[...]), split(values), ((1,), (0,)))
    data[rows, re], data[rows, im] = times((values[:48], values[48:]), turn)
    along_lanes((inverse_hi, inverse_lo))

    lead = lax.broadcasted_iota(jnp.int32, (16, 128), 0) == 0
    for field in range(FIELDS):
        done = []
        for z0 in range(2):
            for l in range(2):
                rows = pl.ds(EXTRA + 16 * field + 8 * z0 + 4 * l, 4)
                extra = data[rows, re] * cos_x - data[rows, im] * sin_x
                reals, imags = [], []
                for cl in range(4):
                    rows = pl.ds(48 * (8 * z0 + 4 * l + cl) + 16 * field, 16)
                    x, y = data[rows, re], data[rows, im]
                    reals.append(x * cos_m - y * sin_m)
                    imags.append(jnp.where(lead, extra[cl : cl + 1], y * cos_m + x * sin_m))
                done.append(jnp.concatenate(reals + imags, axis=0).T)
        for l in range(2):
            for bl in range(2):
                parts = [d[64 * bl : 64 * bl + 64].reshape(8, 1, 8, 128) for d in done[l::2]]
                block = jnp.concatenate(parts, axis=1).reshape(128, 128)
                out[pl.ds(6 * l + field * 2 + bl, 128, stride=12), :] = block


VMEM = pl.BlockSpec(memory_space=pltpu.VMEM)


def call(body, operands, in_specs, shapes, out_specs, scratch=(), limit=24 << 20):
    return pl.pallas_call(
        body,
        out_shape=shapes,
        in_specs=in_specs,
        out_specs=out_specs,
        scratch_shapes=scratch,
        compiler_params=pltpu.CompilerParams(vmem_limit_bytes=limit),
    )(*operands)


WIDE = jax.ShapeDtypeStruct((1536, LANES), jnp.float32)
OWN = jax.ShapeDtypeStruct((512, LANES), jnp.float32)


def run_pack(signal, kernel, gate, grad):
    return call(pack_kernel, (signal, kernel, gate, grad), [VMEM] * 4, WIDE, VMEM)


def run_channel(arrived):
    constants = tables()[:-2]
    scratch = [pltpu.VMEM((ROWS, 256), jnp.float32)]
    specs = [VMEM] * (1 + len(constants))
    return call(channel_kernel, (arrived, *constants), specs, WIDE, VMEM, scratch)


def run_unpack(arrived, gate, grad):
    operands = (arrived, *tables()[-2:], gate, grad)
    return call(unpack_kernel, operands, [VMEM] * 5, (OWN,) * 4, (VMEM,) * 4)


def flat(x):
    return x.reshape(32, 2, 4, 2, LANES).transpose(0, 1, 3, 2, 4).reshape(512, LANES)


def unflat(x):
    return x.reshape(32, 2, 2, 4, LANES).transpose(0, 1, 3, 2, 4).reshape(32, 2, 4, 256)


def exchange(x):
    x = x.reshape(256, FIELDS, 2, LANES)
    x = lax.all_to_all(
        x, ("rows", "cols"), split_axis=0, concat_axis=0, tiled=True, axis_index_groups=[LISTED]
    )
    return x.reshape(1536, LANES)


def shards(signal, kernel, gate_values, grad_out):
    inputs = [flat(x) for x in (signal, kernel, gate_values, grad_out)]
    stored = [pltpu.with_memory_space_constraint(x, pltpu.HBM) for x in inputs]
    done = exchange(run_channel(exchange(run_pack(*stored))))
    return tuple(unflat(x) for x in run_unpack(done, *inputs[2:]))


def solution(mesh):
    place = P(None, "cols", "rows", None)
    return jax.shard_map(
        shards, mesh=mesh, in_specs=(place,) * 4, out_specs=(place,) * 4, check_vma=False
    )
```

```python
import functools

import jax
import jax.numpy as jnp
import ml_dtypes
import numpy as np
from jax import lax
from jax.experimental import pallas as pl
from jax.experimental.pallas import tpu as pltpu
from jax.sharding import PartitionSpec as P

LENGTH = 65536
LISTED = [
    (2 * z + l) * 16 + 8 * h + 2 * x + core
    for z in range(8)
    for core in range(2)
    for x in range(4)
    for h in range(2)
    for l in range(2)
]
LANES = 128
FIELDS = 3
EXTRA = 768
ROWS = EXTRA + 48
CHUNK = 480
SCALE = 1.0 / (65536.0 * 256.0)
HALF = jnp.bfloat16


def halves(table):
    high = table.astype(np.float32).astype(ml_dtypes.bfloat16)
    low = (table - high.astype(np.float64)).astype(np.float32).astype(ml_dtypes.bfloat16)
    return high, low


def tall(table):
    return np.concatenate(np.split(table, 2, axis=1))


@functools.lru_cache(maxsize=None)
def tables():
    a = np.arange(32)
    fa = np.arange(16)
    angle = 2.0 * np.pi * (fa[:, None] * a[None, :] % 32) / 32.0
    first = np.zeros((144, 128))
    last = np.zeros((128, 128))
    weight = np.where(fa == 0, 1.0, 2.0)[:, None] * SCALE
    for cl in range(4):
        columns = slice(32 * cl, 32 * cl + 32)
        first[16 * cl : 16 * cl + 16, columns] = np.cos(angle)
        first[64 + 16 * cl : 64 + 16 * cl + 16, columns] = -np.sin(angle)
        first[128 + cl, columns] = np.where(a % 2 == 0, 1.0, -1.0)
        last[16 * cl : 16 * cl + 16, columns] = weight * np.cos(angle)
        last[64 + 16 * cl : 64 + 16 * cl + 16, columns] = -weight * np.sin(angle)
        last[64 + 16 * cl, columns] = np.where(a % 2 == 0, SCALE, -SCALE)
    last = last.T.reshape(4, 32, 128)
    last = np.stack([np.kron([1.0, 0.0], last), np.kron([0.0, 1.0], last)]).transpose(2, 0, 1, 3).reshape(256, 256)
    first = first.reshape(144, 4, 2, 16).transpose(0, 3, 2, 1).reshape(144, 128)
    lane = np.arange(128)
    q = 8 * (lane % 2) + 2 * (lane // 2 % 4) + lane // 8 % 2
    m = 8 * q + 4 * (lane // 64) + lane // 16 % 4
    g0 = np.arange(128)
    angle = 2.0 * np.pi * (m[:, None] * g0[None, :] % 128) / 128.0
    middle = np.block([[np.cos(angle), -np.sin(angle)], [np.sin(angle), np.cos(angle)]])
    c16 = np.arange(16)
    angle = 2.0 * np.pi * (c16[:, None] * c16[None, :] % 16) / 16.0
    cosine, sine = (np.kron(np.eye(FIELDS), part) for part in (np.cos(angle), np.sin(angle)))
    extra = np.block([[cosine, sine], [-sine, cosine]])
    fa = np.arange(17)
    phase = 2.0 * np.pi * (16 * fa[:, None] * m[None, :] % LENGTH) / LENGTH
    turn_m = np.zeros((2, 24, 128), np.float32)
    turn_m[0, :17] = np.cos(phase)
    turn_m[1, :17] = np.sin(phase)
    phase = c16[:, None, None] * (fa[None, :, None] + 32 * g0[None, None, :]) % LENGTH
    phase = 2.0 * np.pi * phase / LENGTH
    turn_c = np.stack([np.cos(phase), np.sin(phase)]).astype(np.float32)
    turn_x = np.tile(turn_c[:, :, 16], (1, FIELDS, 1))
    turn_c = np.ascontiguousarray(turn_c[:, :, :16])
    return (
        *halves(first), *halves(tall(middle)), *halves(tall(middle.T)), *halves(extra), *halves(extra.T), turn_m, turn_c, turn_x, *halves(tall(last))
    )


def split(values):
    high = values.astype(HALF)
    return high, (values - high.astype(jnp.float32)).astype(HALF)


def product(left, right, dims):
    def one(x, y):
        return lax.dot_general(x, y, (dims, ((), ())), preferred_element_type=jnp.float32)

    return one(left[0], right[0]) + (one(left[0], right[1]) + one(left[1], right[0]))


def sixteen(values, sign):
    def add(x, y):
        return (x[0] + y[0], x[1] + y[1])

    def sub(x, y):
        return (x[0] - y[0], x[1] - y[1])

    def quarter(x):
        return (-x[1], x[0]) if sign > 0 else (x[1], -x[0])

    def four(v):
        s, d = add(v[0], v[2]), sub(v[0], v[2])
        t, u = add(v[1], v[3]), quarter(sub(v[1], v[3]))
        return [add(s, t), add(d, u), sub(s, t), sub(d, u)]

    def turned(x, k):
        if k == 0:
            return x
        if k == 4:
            return quarter(x)
        cosine, sine = float(np.cos(np.pi * k / 8)), float(sign * np.sin(np.pi * k / 8))
        return (x[0] * cosine - x[1] * sine, x[0] * sine + x[1] * cosine)

    inner = [four(values[n::4]) for n in range(4)]
    outer = [four([turned(inner[n][k], n * k) for n in range(4)]) for k in range(4)]
    return [outer[k % 4][k // 4] for k in range(16)]


def times(x, y):
    return (x[0] * y[0] - x[1] * y[1], x[0] * y[1] + x[1] * y[0])


def times_conj(x, y):
    return (x[0] * y[0] + x[1] * y[1], x[1] * y[0] - x[0] * y[1])


def pack_kernel(signal, kernel, gate, grad, out):
    for field in range(FIELDS):
        block = signal[...] if field == 0 else kernel[...] if field == 1 else gate[...] * grad[...]
        block = block.reshape(2, 16, 2, 8, 128)
        for half in range(2):
            for bl in range(2):
                parts = [block[k, :, bl, 4 * half : 4 * half + 4] for k in range(2)]
                part = jnp.concatenate(parts, axis=1).reshape(128, 128)
                out[pl.ds(768 * half + field * 2 + bl, 128, stride=6), :] = part.T


def unpack_kernel(arrived, last_hi, last_lo, gate, grad, gated, signal_grad, kernel_grad, gate_grad):
    last = [jnp.concatenate([ref[0:256, :], ref[256:512, :]], axis=1) for ref in (last_hi, last_lo)]
    for field in range(FIELDS):
        block = [
            [arrived[pl.ds(768 * half + field * 2 + bl, 128, stride=6), :] for half in range(2)]
            for bl in range(2)
        ]
        block = jnp.concatenate([jnp.concatenate(b, axis=1) for b in block], axis=0)
        block = product(last, split(block), ((1,), (1,)))
        for a in range(32):
            for bl in range(2):
                rows = pl.ds(16 * a + 8 * bl, 8)
                part = block[8 * a : 8 * a + 8, 128 * bl : 128 * bl + 128]
                if field == 0:
                    gated[rows, :] = gate[rows, :] * part
                    gate_grad[rows, :] = grad[rows, :] * part
                elif field == 1:
                    signal_grad[rows, :] = part
                else:
                    kernel_grad[rows, :] = part


def channel_kernel(
    arrived, first_hi, first_lo, middle_hi, middle_lo, inverse_hi, inverse_lo, extra_hi, extra_lo, back_hi, back_lo, turn_m, turn_c, turn_x,
    out, data,
):
    re, im = slice(0, 128), slice(128, 256)
    cos_m, sin_m = turn_m[0, 0:16], turn_m[1, 0:16]
    cos_x, sin_x = turn_m[0, 16:17], turn_m[1, 16:17]
    first = (first_hi[...], first_lo[...])
    for field in range(FIELDS):
        blocks = [
            arrived[pl.ds(6 * l + field * 2 + bl, 128, stride=12), :].reshape(4, 2, 16, 128)
            for l in range(2)
            for bl in range(2)
        ]
        for z0 in range(2):
            block = jnp.concatenate([b[:, z0].reshape(64, 128) for b in blocks], axis=0)
            mixed = product(first, split(block), ((1,), (1,)))
            for l in range(2):
                lanes = slice(128 * l, 128 * l + 128)
                for cl in range(4):
                    rows = pl.ds(48 * (8 * z0 + 4 * l + cl) + 16 * field, 16)
                    x, y = mixed[16 * cl : 16 * cl + 16, lanes], mixed[64 + 16 * cl : 80 + 16 * cl, lanes]
                    data[rows, re] = x * cos_m + y * sin_m
                    data[rows, im] = y * cos_m - x * sin_m
                rows = pl.ds(EXTRA + 16 * field + 8 * z0 + 4 * l, 4)
                x = mixed[128:132, lanes]
                data[rows, re] = x * cos_x
                data[rows, im] = -(x * sin_x)

    def along_lanes(refs):
        table = [jnp.concatenate([ref[0:256, :], ref[256:512, :]], axis=1) for ref in refs]
        for start in range(0, ROWS, CHUNK):
            rows = pl.ds(start, min(CHUNK, ROWS - start))
            data[rows, :] = product(split(data[rows, :]), table, ((1,), (0,)))

    def multiply(spectra):
        signal, kernel, grad = spectra
        return (
            [times(s, k) for s, k in zip(signal, kernel)],
            [times_conj(g, k) for g, k in zip(grad, kernel)],
            [times_conj(g, s) for g, s in zip(grad, signal)],
        )

    along_lanes((middle_hi, middle_lo))
    for start in (0, 8):
        turn = [(turn_c[0, c, start : start + 8], turn_c[1, c, start : start + 8]) for c in range(16)]
        spectra = []
        for field in range(FIELDS):
            rows = [pl.ds(start + 16 * field + 48 * c, 8) for c in range(16)]
            values = [times_conj((data[r, re], data[r, im]), t) for r, t in zip(rows, turn)]
            spectra.append(sixteen(values, -1))
        for field, result in enumerate(multiply(spectra)):
            for c, (v, t) in enumerate(zip(sixteen(result, 1), turn)):
                rows = pl.ds(start + 16 * field + 48 * c, 8)
                data[rows, re], data[rows, im] = times(v, t)
    rows, turn = pl.ds(EXTRA, 48), (turn_x[0], turn_x[1])
    extra = (extra_hi[...], extra_lo[...])
    values = jnp.concatenate(times_conj((data[rows, re], data[rows, im]), turn), axis=0)
    values = product(extra, split(values), ((1,), (0,)))
    spectra = [[(values[16 * f : 16 * f + 16], values[48 + 16 * f : 64 + 16 * f])] for f in range(FIELDS)]
    results = multiply(spectra)
    values = jnp.concatenate([result[0][part] for part in range(2) for result in results], axis=0)
    values = product((back_hi[...], back_lo[...]), split(values), ((1,), (0,)))
    data[rows, re], data[rows, im] = times((values[:48], values[48:]), turn)
    along_lanes((inverse_hi, inverse_lo))

    lead = lax.broadcasted_iota(jnp.int32, (16, 128), 0) == 0
    for field in range(FIELDS):
        done = []
        for z0 in range(2):
            for l in range(2):
                rows = pl.ds(EXTRA + 16 * field + 8 * z0 + 4 * l, 4)
                extra = data[rows, re] * cos_x - data[rows, im] * sin_x
                reals, imags = [], []
                for cl in range(4):
                    rows = pl.ds(48 * (8 * z0 + 4 * l + cl) + 16 * field, 16)
                    x, y = data[rows, re], data[rows, im]
                    reals.append(x * cos_m - y * sin_m)
                    imags.append(jnp.where(lead, extra[cl : cl + 1], y * cos_m + x * sin_m))
                done.append(jnp.concatenate(reals + imags, axis=0).T)
        for l in range(2):
            for bl in range(2):
                parts = [d[64 * bl : 64 * bl + 64].reshape(4, 1, 16, 128) for d in done[l::2]]
                block = jnp.concatenate(parts, axis=1).reshape(128, 128)
                out[pl.ds(6 * l + field * 2 + bl, 128, stride=12), :] = block


VMEM = pl.BlockSpec(memory_space=pltpu.VMEM)


def call(body, operands, in_specs, shapes, out_specs, scratch=(), limit=24 << 20):
    return pl.pallas_call(
        body,
        out_shape=shapes,
        in_specs=in_specs,
        out_specs=out_specs,
        scratch_shapes=scratch,
        compiler_params=pltpu.CompilerParams(vmem_limit_bytes=limit),
    )(*operands)


WIDE = jax.ShapeDtypeStruct((1536, LANES), jnp.float32)
OWN = jax.ShapeDtypeStruct((512, LANES), jnp.float32)


def run_pack(signal, kernel, gate, grad):
    return call(pack_kernel, (signal, kernel, gate, grad), [VMEM] * 4, WIDE, VMEM)


def run_channel(arrived):
    constants = tables()[:-2]
    scratch = [pltpu.VMEM((ROWS, 256), jnp.float32)]
    specs = [VMEM] * (1 + len(constants))
    return call(channel_kernel, (arrived, *constants), specs, WIDE, VMEM, scratch)


def run_unpack(arrived, gate, grad):
    operands = (arrived, *tables()[-2:], gate, grad)
    return call(unpack_kernel, operands, [VMEM] * 5, (OWN,) * 4, (VMEM,) * 4)


def flat(x):
    return x.reshape(32, 2, 4, 2, LANES).transpose(0, 1, 3, 2, 4).reshape(512, LANES)


def unflat(x):
    return x.reshape(32, 2, 2, 4, LANES).transpose(0, 1, 3, 2, 4).reshape(32, 2, 4, 256)


def exchange(x):
    x = x.reshape(256, FIELDS, 2, LANES)
    x = lax.all_to_all(
        x, ("rows", "cols"), split_axis=0, concat_axis=0, tiled=True, axis_index_groups=[LISTED]
    )
    return x.reshape(1536, LANES)


def shards(signal, kernel, gate_values, grad_out):
    inputs = [flat(x) for x in (signal, kernel, gate_values, grad_out)]
    stored = [pltpu.with_memory_space_constraint(x, pltpu.HBM) for x in inputs]
    done = exchange(run_channel(exchange(run_pack(*stored))))
    return tuple(unflat(x) for x in run_unpack(done, *inputs[2:]))


def solution(mesh):
    place = P(None, "cols", "rows", None)
    return jax.shard_map(
        shards, mesh=mesh, in_specs=(place,) * 4, out_specs=(place,) * 4, check_vma=False
    )
```
